128 devices in a mesh: net: 16 (over y, x), line: 8 (over z, core).
Axes of the slice: x: 4, y: 4, z: 4, core: 2. Of those that a mesh axis runs over, the one named last changes fastest.
Arguments:
- inverses: float32 [512, 1024, 1024], P('net', 'line'), as said below
- node_counts: int32 [512], P('net'), may hold values from 384 to 1024, as said below
- sources: float32 [16, 512, 1024], P(None, 'net'), may hold values from -6 to 6
- port_slot: int32 [512, 64], P('net', 'line'), may hold values from 0 to 1023, as said below
- end_slot: int32 [2, 16384], P(None, ('net', 'line')), may hold values from 0 to 1023, as said below
- modal_map: float32 [6, 6, 16384], P(None, None, ('net', 'line')), may hold values from -1 to 1
- delay_steps: int32 [6, 16384], P(None, ('net', 'line')), may hold values from 1 to 64
- wave_buffer: float32 [2, 6, 64, 16384], P(None, None, None, ('net', 'line')), may hold values from -6 to 6
- yc_decay: float32 [6, 30, 16384], P(None, None, ('net', 'line')), may hold values from 0.2 to 0.99
- yc_residue: float32 [6, 30, 16384], P(None, None, ('net', 'line')), may hold values from -0.04 to 0.04
- yc_direct: float32 [6, 16384], P(None, ('net', 'line')), may hold values from 0.25 to 1
- yc_state: float32 [2, 6, 30, 16384], P(None, None, None, ('net', 'line')), may hold values from -0.6 to 0.6
- prop_decay: float32 [6, 30, 16384], P(None, None, ('net', 'line')), may hold values from 0.2 to 0.99
- prop_residue: float32 [6, 30, 16384], P(None, None, ('net', 'line')), may hold values from 0 to 0.008
- prop_state: float32 [2, 6, 30, 16384], P(None, None, None, ('net', 'line')), may hold values from -0.6 to 0.6
Outputs:
- node_volts: float32 [16, 512, 1024], P(None, 'net', 'line')
- line_currents: float32 [16, 2, 6, 16384], P(None, None, None, ('net', 'line'))
The draws below stay inside these ranges and needn't reach their ends.
Inputs may be any that keep to these rules, and one draw needn't show every extreme that they name: `inverses`: rows and columns at and past node_counts of a subnetwork are zero. `node_counts`: some subnetwork has 1024 nodes and some has 384. port_slot // 8 is the device along net+line that holds the joined line end and port_slot % 8 a slot; the ports held by one device name distinct values, and in every draw some device fills all 8 slots of some other device. end_slot // 8 is the device along net+line that holds the joined port and end_slot % 8 the same slot; the line ends held by one device name distinct values, and in every draw some device receives 8 of them from one other device.
All inputs are finite; a program needn't handle non-finite values.
Results may differ from the reference program's by a relative error of at most 0.0001.
Values sent between devices are 32-bit elements; how exact they have to be, the bound alone decides.
A program may use at most 64 MiB of HBM per device.

```python
import math
import jax
import jax.numpy as jnp
from jax import lax

NODES = 1024
MODES = 6
POLES = 30
PORTS = 64
BUF = 64
STEPS = 16
SUB_DEV = 32
PORT_ROWS = 256
LINE_DEV = 128
CAP = 8
HEAVY = 19
SUBS = 512
LINES = 16384
N_NET = 16
N_LINE = 8


def shuffled_rows(base, device_count, count):
    keys = jax.random.split(base, device_count)
    return jax.vmap(lambda sub_key: jax.random.permutation(sub_key, count))(keys)


def joined_slots(key):
    device_count = N_NET * N_LINE
    row_total = PORT_ROWS
    relabel = jax.random.permutation(jax.random.fold_in(key, 11), device_count).astype(jnp.int32)
    position = jnp.argsort(relabel).astype(jnp.int32)
    shifts = jax.random.permutation(jax.random.fold_in(key, 12), device_count).astype(jnp.int32)
    row_ids = jnp.arange(row_total, dtype=jnp.int32)
    heavy_rows = row_ids < HEAVY * CAP
    shift_of = jnp.where(heavy_rows, row_ids // CAP, HEAVY + row_ids - HEAVY * CAP)
    slot_of = jnp.where(heavy_rows, row_ids % CAP, 0)
    shuffled = shuffled_rows(jax.random.fold_in(key, 13), device_count, row_total)
    senders = jnp.arange(device_count, dtype=jnp.int32)[:, None]
    targets = relabel[(position[senders] + shifts[shift_of[shuffled]]) % device_count]
    slots = slot_of[shuffled]
    send_code = targets * CAP + slots
    recv_code = senders * CAP + slots
    order_key = (targets * (device_count * CAP) + recv_code).reshape(-1)
    ranked = jnp.argsort(order_key, stable=True)
    arriving = recv_code.reshape(-1)[ranked].reshape(device_count, row_total)
    spread = shuffled_rows(jax.random.fold_in(key, 14), device_count, row_total)
    placed = jnp.take_along_axis(arriving, spread, axis=1)
    end_table = placed.reshape(device_count, 2, LINE_DEV).transpose(1, 0, 2).reshape(2, LINES)
    port_table = send_code.reshape(N_NET, N_LINE, SUB_DEV, PORTS // N_LINE).transpose(0, 2, 1, 3).reshape(SUBS, PORTS)
    return (port_table.astype(jnp.int32), end_table.astype(jnp.int32))


def node_sizes(key):
    lowest = MODES * PORTS
    counts = jax.random.randint(jax.random.fold_in(key, 21), (SUBS,), lowest, NODES + 1, dtype=jnp.int32)
    return counts.at[0].set(NODES).at[1].set(lowest)


def pole_rates(key, salt):
    return jax.random.uniform(jax.random.fold_in(key, salt), (MODES, POLES, LINES), jnp.float32, 0.2, 0.99)


def draw_port_slot(key, part):
    shared = joined_slots(key)
    return shared[0]


def draw_end_slot(key, part):
    shared = joined_slots(key)
    return shared[1]


def draw_node_counts(key, part):
    counts = node_sizes(key)
    return counts


def draw_inverses(key, part):
    counts = node_sizes(key)
    key = jax.random.fold_in(key, 3)
    node_ids = jnp.arange(NODES, dtype=jnp.int32)
    inside = (node_ids[None, :] < counts[:, None]).astype(jnp.float32)
    diagonal = jnp.exp(jax.random.uniform(jax.random.fold_in(key, 1), (SUBS, NODES), jnp.float32, math.log(0.5), math.log(2.0)))
    spread = jax.random.normal(jax.random.fold_in(key, 2), (SUBS, NODES, NODES), jnp.float32) * (0.5 / math.sqrt(NODES))
    identity = (node_ids[:, None] == node_ids[None, :]).astype(jnp.float32)
    full = spread + identity[None] * diagonal[:, :, None]
    return full * inside[:, :, None] * inside[:, None, :]


def draw_delay_steps(key, part):
    key = jax.random.fold_in(key, 4)
    delays = jax.random.randint(key, (MODES, LINES), 1, BUF + 1, dtype=jnp.int32)
    return delays.at[0, 0].set(BUF).at[0, 1].set(1)


def draw_modal_map(key, part):
    key = jax.random.fold_in(key, 8)
    magnitude = jax.random.uniform(jax.random.fold_in(key, 1), (MODES, LINES), jnp.float32, 0.5, 1.5)
    positive = jax.random.bernoulli(jax.random.fold_in(key, 2), 0.5, (MODES, LINES))
    vector = magnitude * jnp.where(positive, 1.0, -1.0).astype(jnp.float32)
    length_sq = jnp.sum(vector * vector, axis=0)
    identity = jnp.eye(MODES, dtype=jnp.float32)[:, :, None]
    return identity - 2.0 * vector[:, None, :] * vector[None, :, :] / length_sq[None, None, :]


def draw_yc_decay(key, part):
    rates = pole_rates(key, 32)
    return rates


def draw_yc_residue(key, part):
    rates = pole_rates(key, 32)
    key = jax.random.fold_in(key, 10)
    weights = jax.random.uniform(key, (MODES, POLES, LINES), jnp.float32, -0.05, 0.05)
    return (1.0 - rates) * weights


def draw_prop_decay(key, part):
    rates = pole_rates(key, 31)
    return rates


def draw_prop_residue(key, part):
    rates = pole_rates(key, 31)
    key = jax.random.fold_in(key, 7)
    weights = jax.random.uniform(key, (MODES, POLES, LINES), jnp.float32, 0.0, 0.01)
    return (1.0 - rates) * weights


def block_scale(own_key, extent, cuts, low, largest):
    def one(dim, parts):
        draws = jax.random.uniform(jax.random.fold_in(jax.random.fold_in(own_key, 6), dim), (parts,), jnp.float32, low / len(cuts), largest / len(cuts))
        return jnp.repeat(jnp.exp(draws), extent[dim] // parts).reshape((-1,) + (1,) * (len(extent) - dim - 1))

    factor_of = one(*cuts[0])
    for cut in cuts[1:]:
        factor_of = factor_of * one(*cut)
    return factor_of


def bell_draw(key, shape, deviation, reach, shards=(), held_as=jnp.bfloat16):
    loudness = block_scale(key, shape, shards, -0.22, 0.18) if shards else 1.0
    result = jax.random.normal(key, shape, jnp.float32) * deviation * loudness
    return jnp.minimum(jnp.maximum(result, -reach), reach).astype(held_as)


def setup_inputs(seed: int = 0) -> dict:
    arg_keys = jax.random.split(jax.random.key(seed), 16)
    return {
        "inverses": draw_inverses(jax.random.fold_in(arg_keys[15], 71), 0),
        "node_counts": draw_node_counts(jax.random.fold_in(arg_keys[15], 71), 0),
        "sources": bell_draw(arg_keys[2], (STEPS, SUBS, NODES), 1.0, 6.0, ((1, 16),), jnp.float32),
        "port_slot": draw_port_slot(jax.random.fold_in(arg_keys[15], 71), 0),
        "end_slot": draw_end_slot(jax.random.fold_in(arg_keys[15], 71), 0),
        "modal_map": draw_modal_map(jax.random.fold_in(arg_keys[15], 71), 0),
        "delay_steps": draw_delay_steps(jax.random.fold_in(arg_keys[15], 71), 0),
        "wave_buffer": bell_draw(arg_keys[7], (2, MODES, BUF, LINES), 1.0, 6.0, ((3, 128),), jnp.float32),
        "yc_decay": draw_yc_decay(jax.random.fold_in(arg_keys[15], 71), 0),
        "yc_residue": draw_yc_residue(jax.random.fold_in(arg_keys[15], 71), 0),
        "yc_direct": jnp.clip(jnp.exp(math.log(1.0) - 1.3862944 * jax.random.uniform(arg_keys[10], (MODES, LINES), jnp.float32) ** block_scale(arg_keys[10], (MODES, LINES), ((1, 128),), -0.2, 0.2)), 0.25, 1.0),
        "yc_state": bell_draw(arg_keys[11], (2, MODES, POLES, LINES), 0.1, 0.6, ((3, 128),), jnp.float32),
        "prop_decay": draw_prop_decay(jax.random.fold_in(arg_keys[15], 71), 0),
        "prop_residue": draw_prop_residue(jax.random.fold_in(arg_keys[15], 71), 0),
        "prop_state": bell_draw(arg_keys[14], (2, MODES, POLES, LINES), 0.1, 0.6, ((3, 128),), jnp.float32),
    }


def read_delayed(extended, delay_steps, step_index, buffer_len):
    read_at = buffer_len + step_index - delay_steps
    depth = jnp.arange(extended.shape[2], dtype=jnp.int32)
    picker = (depth[None, :, None] == read_at[:, None, :]).astype(extended.dtype)
    return jnp.sum(extended * picker[None], axis=2)


def reference(inverses, node_counts, sources, port_slot, end_slot, modal_map, delay_steps, wave_buffer, yc_decay, yc_residue, yc_direct, yc_state, prop_decay, prop_residue, prop_state):
    device_count = N_NET * N_LINE
    slot_width = device_count * CAP
    port_ids = jnp.arange(SUBS * PORTS, dtype=jnp.int32)
    sub_of = port_ids // PORTS
    port_of = port_ids % PORTS
    sender = (sub_of // SUB_DEV) * N_LINE + port_of // (PORTS // N_LINE)
    port_key = sender * slot_width + port_slot.reshape(-1)
    line_ids = jnp.arange(LINES, dtype=jnp.int32)
    holder = line_ids // LINE_DEV
    end_key = (end_slot // CAP) * slot_width + holder[None, :] * CAP + end_slot % CAP
    table = jnp.zeros((device_count * slot_width,), jnp.int32).at[port_key].set(port_ids)
    port_of_end = table[end_key.reshape(-1)]
    back_table = jnp.zeros((device_count * slot_width,), jnp.int32).at[end_key.reshape(-1)].set(jnp.arange(2 * LINES, dtype=jnp.int32))
    end_of_port = back_table[port_key]
    node_ids = jnp.arange(NODES, dtype=jnp.int32)
    live_mask = node_ids[None, :] < node_counts[:, None]
    used_nodes = PORTS * MODES
    extended = jnp.concatenate([wave_buffer, jnp.zeros((2, MODES, STEPS, LINES), wave_buffer.dtype)], axis=2)
    yc_now = yc_state
    prop_now = prop_state
    volts_list = []
    currents_list = []
    for step_index in range(STEPS):
        delayed = read_delayed(extended, delay_steps, step_index, BUF)
        prop_now = prop_decay[None] * prop_now + prop_residue[None] * delayed[::-1][:, :, None, :]
        history = jnp.sum(prop_now, axis=2)
        history_phase = jnp.sum(modal_map[None] * history[:, None], axis=2)
        flat_history = history_phase.transpose(0, 2, 1).reshape(2 * LINES, MODES)
        port_currents = flat_history[end_of_port].reshape(SUBS, PORTS, MODES).transpose(0, 2, 1).reshape(SUBS, used_nodes)
        injection = sources[step_index] + jnp.pad(port_currents, ((0, 0), (0, NODES - used_nodes)))
        solved = jnp.einsum("src,sc->sr", inverses, injection, precision=lax.Precision.HIGHEST)
        solved = jnp.where(live_mask, solved, 0.0)
        port_volts = solved[:, :used_nodes].reshape(SUBS, MODES, PORTS).transpose(0, 2, 1).reshape(SUBS * PORTS, MODES)
        end_volts = port_volts[port_of_end].reshape(2, LINES, MODES).transpose(2, 0, 1)
        modal_volts = jnp.sum(modal_map[:, :, None, :] * end_volts[:, None], axis=0).transpose(1, 0, 2)
        yc_now = yc_decay[None] * yc_now + yc_residue[None] * modal_volts[:, :, None, :]
        charac = yc_direct[None] * modal_volts + jnp.sum(yc_now, axis=2)
        current = charac - history
        wave_out = 2.0 * charac - history
        extended = extended.at[:, :, BUF + step_index, :].set(wave_out)
        volts_list.append(solved)
        currents_list.append(current)
    return jnp.stack(volts_list), jnp.stack(currents_list)
```

```python
import functools
import jax
import jax.numpy as jnp
from jax import lax
from jax.experimental import pallas as pl
from jax.experimental.pallas import tpu as pltpu
from jax.sharding import PartitionSpec as P

MESH = pl.DeviceIdType.MESH
VMEM_CAP = 56 * 1024 * 1024
DEVICES = 128
SLOTS = 16
ENDS = 256
RING = (0, 1, 2, 1)
OFFSETS = sorted(
    [(a, b, c, e) for a in range(4) for b in range(4) for c in range(4) for e in range(2) if (a, b, c, e) != (0, 0, 0, 0)],
    key=lambda o: -(RING[o[0]] + RING[o[1]] + RING[o[2]] + o[3]),
)


def place():
    i = lax.axis_index("net")
    z = lax.axis_index("line")
    return i, z


def peer(i, z, offset):
    dy, dx, dz, dc = offset
    y, x, zz, c = i // 4, lax.rem(i, 4), z // 2, lax.rem(z, 2)
    ni = lax.rem(y + dy, 4) * 4 + lax.rem(x + dx, 4)
    nz = lax.rem(zz + dz, 4) * 2 + lax.rem(c + dc, 2)
    return ni, nz


def greet_all(i, z):
    barrier = pltpu.get_barrier_semaphore()
    for offset in OFFSETS:
        pl.semaphore_signal(barrier, inc=1, device_id=peer(i, z, offset), device_id_type=MESH)
    pl.semaphore_wait(barrier, len(OFFSETS))


def drain(ref, count, sem):
    part = ref.at[pl.ds(0, count)]
    pltpu.make_async_copy(part, part, sem).wait()


def swap_all_kernel(x_ref, o_ref, send_sem, recv_sem, own_sem):
    i, z = place()
    me = i * 8 + z
    greet_all(i, z)
    own = pltpu.make_async_copy(x_ref.at[me], o_ref.at[me], own_sem)
    own.start()
    for offset in OFFSETS:
        ni, nz = peer(i, z, offset)
        pltpu.make_async_remote_copy(
            src_ref=x_ref.at[ni * 8 + nz], dst_ref=o_ref.at[me], send_sem=send_sem, recv_sem=recv_sem,
            device_id=(ni, nz), device_id_type=MESH,
        ).start()
    own.wait()
    drain(o_ref, DEVICES - 1, recv_sem)
    drain(x_ref, DEVICES - 1, send_sem)


def swap_line_kernel(x_ref, o_ref, send_sem, recv_sem, own_sem):
    i, z = place()
    barrier = pltpu.get_barrier_semaphore()
    for k in range(1, 8):
        pl.semaphore_signal(barrier, inc=1, device_id=(i, lax.rem(z + k, 8)), device_id_type=MESH)
    pl.semaphore_wait(barrier, 7)
    own = pltpu.make_async_copy(x_ref.at[z], o_ref.at[z], own_sem)
    own.start()
    for k in range(1, 8):
        nz = lax.rem(z + k, 8)
        pltpu.make_async_remote_copy(
            src_ref=x_ref.at[nz], dst_ref=o_ref.at[z], send_sem=send_sem, recv_sem=recv_sem,
            device_id=(i, nz), device_id_type=MESH,
        ).start()
    own.wait()
    drain(o_ref, 7, recv_sem)
    drain(x_ref, 7, send_sem)


def swap(kernel, x, collective_id, name):
    return pl.pallas_call(
        kernel,
        out_shape=jax.ShapeDtypeStruct(x.shape, x.dtype),
        in_specs=[pl.BlockSpec(memory_space=pl.ANY)],
        out_specs=pl.BlockSpec(memory_space=pl.ANY),
        scratch_shapes=[pltpu.SemaphoreType.DMA] * 3,
        compiler_params=pltpu.CompilerParams(collective_id=collective_id, has_side_effects=True),
        name=name,
    )(x)


def response_kernel(
    yd, yr, ydir, ys_in, pd, pr, ps_in, delay, waves, hist0, zero_in, ht, g, yst, pst, yim, pim, hbuf
):
    steps = hist0.shape[1]
    yst[...] = ys_in[...]
    pst[...] = ps_in[...]
    yim[...] = yr[...]
    pim[...] = pr[...]
    depth = lax.broadcasted_iota(jnp.int32, (6, 64, 128), 1)

    def step(n, carry):
        pick = depth == (64 + n - delay[...])[:, None, :]
        ydec, pdec, pres = yd[...], pd[...], pr[...]
        for e in range(2):
            seen = jnp.sum(jnp.where(pick, waves[1 - e], 0.0), axis=1)
            now = pdec * pst[e] + pres * seen[:, None, :]
            pst[e] = now
            hist0[e, n] = jnp.sum(now, axis=1)
            free = ydec * yst[e]
            yst[e] = free
            zero_in[e, n] = jnp.sum(free, axis=1)
        first = jnp.where(n == 0, 1.0, 0.0)
        pnow, ynow = pim[...], yim[...]
        hbuf[n] = jnp.sum(pnow, axis=1)
        g[n] = jnp.sum(ynow, axis=1) + first * ydir[...]
        pim[...] = pnow * pdec
        yim[...] = ynow * ydec
        return carry

    lax.fori_loop(0, steps, step, 0)
    lag = delay[...]
    ht[0] = jnp.zeros((6, 128), jnp.float32)
    for k in range(1, steps):
        total = jnp.zeros((6, 128), jnp.float32)
        for m in range(k):
            total = total + jnp.where(lag == k - m, hbuf[m], 0.0)
        ht[k] = total


def line_responses(yc_decay, yc_residue, yc_direct, yc_state, prop_decay, prop_residue, prop_state, delay_steps, wave_buffer):
    two = jax.ShapeDtypeStruct((2, 16, 6, 128), jnp.float32)
    one = jax.ShapeDtypeStruct((16, 6, 128), jnp.float32)
    vm = pl.BlockSpec(memory_space=pltpu.VMEM)
    return pl.pallas_call(
        response_kernel,
        out_shape=(two, two, one, one),
        in_specs=[vm] * 9,
        out_specs=(vm,) * 4,
        scratch_shapes=[
            pltpu.VMEM((2, 6, 30, 128), jnp.float32),
            pltpu.VMEM((2, 6, 30, 128), jnp.float32),
            pltpu.VMEM((6, 30, 128), jnp.float32),
            pltpu.VMEM((6, 30, 128), jnp.float32),
            pltpu.VMEM((16, 6, 128), jnp.float32),
        ],
        compiler_params=pltpu.CompilerParams(vmem_limit_bytes=VMEM_CAP),
        name="line_responses",
    )(yc_decay, yc_residue, yc_direct, yc_state, prop_decay, prop_residue, prop_state, delay_steps, wave_buffer)


def split(value):
    high = value.astype(jnp.bfloat16)
    low = (value - high.astype(jnp.float32)).astype(jnp.bfloat16)
    return high, low


def steps_kernel(
    inverses, v0_send, hist_in, zero_in, ht, g, mmap, send_rank, send_dev, recv_rank, recv_dev, over_in,
    inject_out, current_out, flag_out,
    block, v0, solve, hacc, cacc, to_row, from_row, send_buf, recv_buf,
    block_send, block_recv, v0_sendsem, v0_recv, own_sem, wave_send, wave_recv,
):
    i, z = place()
    me = i * 8 + z
    steps = 16
    lane = lax.broadcasted_iota(jnp.int32, (1, 128), 1)
    greet_all(i, z)

    def block_copy(src_z, dst_z):
        return inverses.at[pl.ds(dst_z * 4, 4), :, pl.ds(0, 384)], block.at[src_z]

    @pl.when(z < 3)
    def _send():
        for k in range(1, 8):
            nz = lax.rem(z + k, 8)
            pltpu.make_async_remote_copy(
                src_ref=v0_send.at[nz], dst_ref=v0.at[z], send_sem=v0_sendsem, recv_sem=v0_recv.at[z],
                device_id=(i, nz), device_id_type=MESH,
            ).start()
        for k in range(1, 8):
            nz = lax.rem(z + k, 8)
            src, dst = block_copy(z, nz)
            pltpu.make_async_remote_copy(
                src_ref=src, dst_ref=dst, send_sem=block_send, recv_sem=block_recv.at[z],
                device_id=(i, nz), device_id_type=MESH,
            ).start()
        src, dst = block_copy(z, z)
        own = pltpu.make_async_copy(src, dst, own_sem.at[0])
        own.start()
        own2 = pltpu.make_async_copy(v0_send.at[z], v0.at[z], own_sem.at[1])
        own2.start()
        own.wait()
        own2.wait()

    hacc[...] = jnp.zeros(hacc.shape, jnp.float32)
    cacc[...] = jnp.zeros(cacc.shape, jnp.float32)
    hacc[0:steps] = hist_in[...]
    cacc[0:steps] = zero_in[...]
    to_row[...] = jnp.where(
        lax.broadcasted_iota(jnp.int32, (DEVICES, ENDS), 0) == send_dev[...], 1.0, 0.0
    ).astype(jnp.bfloat16)
    from_row[...] = jnp.where(
        lax.broadcasted_iota(jnp.int32, (ENDS, DEVICES), 1) == recv_dev[...], 1.0, 0.0
    ).astype(jnp.bfloat16)
    mode_pick = jnp.where(
        lax.rem(lax.broadcasted_iota(jnp.int32, (8, 256), 1), 128) // SLOTS
        == lax.broadcasted_iota(jnp.int32, (8, 256), 0), 1.0, 0.0
    ).astype(jnp.bfloat16)

    for src_z in range(3):
        @pl.when(z != src_z)
        def _wait():
            pltpu.make_async_copy(block.at[src_z], block.at[src_z], block_recv.at[src_z]).wait()
            pltpu.make_async_copy(v0.at[src_z], v0.at[src_z], v0_recv.at[src_z]).wait()

    def build(t, carry):
        for src_z in range(3):
            for h in range(2):
                for kk in range(2):
                    rows = block[src_z, t * 2 + h, kk * 64:(kk + 1) * 64, :]
                    row0 = (src_z * 2 + kk) * 128 + h * 64
                    for k in range(6):
                        tile = rows[:, (k // 2) * 128:(k // 2 + 1) * 128]
                        if k % 2 != h:
                            tile = pltpu.roll(tile, 64, 1)
                        tile = jnp.where((lane // 64) == h, tile, 0.0)
                        high, low = split(tile)
                        solve[t, row0:row0 + 64, k * 128:(k + 1) * 128] = high
                        solve[t, 768 + row0:768 + row0 + 64, k * 128:(k + 1) * 128] = low
        return carry

    lax.fori_loop(0, 2, build, 0)

    over = over_in[0:1, 0:1]
    flag_lane = jnp.where(lane == 127, 1.0, 0.0) * over

    def step(n, carry):
        delayed, worst = carry
        par = lax.rem(n, 2)
        hist = hacc[n] + ht[1] * delayed
        phase = [jnp.sum(mmap[k] * hist, axis=0, keepdims=True) for k in range(6)]
        volts = []
        for t in range(2):
            inj = jnp.concatenate([p[:, t * 128:(t + 1) * 128] for p in phase], axis=1)
            inject_out[t, pl.ds(n, 1), :] = inj
            high, low = split(inj)
            left = jnp.concatenate([high, low], axis=0)
            both = lax.dot_general(
                left, solve[t], (((1,), (1,)), ((), ())), preferred_element_type=jnp.float32
            )
            total = jnp.sum(both, axis=0, keepdims=True)
            total = total[:, :768] + total[:, 768:]
            base = jnp.concatenate([v0[a, t, pl.ds(n, 1), :] for a in range(3)], axis=1)
            volts.append(total + base)
        modal = jnp.zeros((8, ENDS), jnp.float32)
        for k in range(6):
            row = jnp.concatenate([v[:, k * 128:(k + 1) * 128] for v in volts], axis=1)
            modal = modal + mmap[k] * row
        charac = cacc[n] + g[0] * modal
        wave = 2.0 * charac - hist
        current_out[n] = charac - hist

        @pl.when(n < steps - 1)
        def _exchange():
            @pl.when(n > 1)
            def _free():
                drain(send_buf.at[par], DEVICES - 1, wave_send.at[par])
            spread = jnp.concatenate(
                [jnp.broadcast_to(wave[j:j + 1], (SLOTS, ENDS)) for j in range(8)], axis=0
            )
            slot = lax.rem(lax.broadcasted_iota(jnp.int32, (DEVICES, ENDS), 0), SLOTS)
            spread = jnp.where(slot == send_rank[...], spread, 0.0)
            high, low = split(spread)
            rows = lax.dot_general(
                to_row[...], jnp.concatenate([high, low], axis=0), (((1,), (1,)), ((), ())),
                preferred_element_type=jnp.float32,
            )
            send_buf[par] = (rows[:, :128] + rows[:, 128:] + flag_lane)[:, None, :]
            for offset in OFFSETS:
                ni, nz = peer(i, z, offset)
                pltpu.make_async_remote_copy(
                    src_ref=send_buf.at[par, ni * 8 + nz], dst_ref=recv_buf.at[par, me],
                    send_sem=wave_send.at[par], recv_sem=wave_recv.at[par],
                    device_id=(ni, nz), device_id_type=MESH,
                ).start()
            recv_buf[par, me] = send_buf[par, me]

        for k in range(2, steps):
            hacc[n + k - 1] = hacc[n + k - 1] + ht[k] * delayed
        for k in range(1, steps):
            cacc[n + k] = cacc[n + k] + g[k] * modal

        @pl.when(n < steps - 1)
        def _arrive():
            drain(recv_buf.at[par], DEVICES - 1, wave_recv.at[par])

        got = recv_buf[par].reshape(DEVICES, 128)
        worst = jnp.maximum(worst, jnp.max(got[:, 127:128], axis=0, keepdims=True))
        high, low = split(got)
        mine = jnp.dot(from_row[...], jnp.concatenate([high, low], axis=1), preferred_element_type=jnp.float32)
        slot = lax.rem(lax.broadcasted_iota(jnp.int32, (ENDS, 256), 1), SLOTS)
        mine = jnp.where(slot == recv_rank[...], mine, 0.0).astype(jnp.bfloat16)
        delayed = lax.dot_general(mode_pick, mine, (((1,), (1,)), ((), ())), preferred_element_type=jnp.float32)
        return delayed, worst

    delayed, worst = lax.fori_loop(
        0, steps, step, (jnp.zeros((8, ENDS), jnp.float32), jnp.zeros((1, 1), jnp.float32))
    )
    flag_out[...] = jnp.broadcast_to(worst, flag_out.shape)
    drain(send_buf.at[0], DEVICES - 1, wave_send.at[0])
    drain(send_buf.at[1], DEVICES - 1, wave_send.at[1])

    @pl.when(z < 3)
    def _sent():
        pltpu.make_async_copy(v0_send.at[pl.ds(0, 7)], v0_send.at[pl.ds(0, 7)], v0_sendsem).wait()
        seven = inverses.at[pl.ds(0, 28), :, pl.ds(0, 384)]
        pltpu.make_async_copy(seven, seven, block_send).wait()


def run_steps(inverses, v0_send, hist, zero_in, ht, g, mmap, send_rank, send_dev, recv_rank, recv_dev, over):
    vm = pl.BlockSpec(memory_space=pltpu.VMEM)
    any_ = pl.BlockSpec(memory_space=pl.ANY)
    f32 = jnp.float32
    dma = pltpu.SemaphoreType.DMA
    return pl.pallas_call(
        steps_kernel,
        out_shape=(
            jax.ShapeDtypeStruct((2, 16, 768), f32),
            jax.ShapeDtypeStruct((16, 8, ENDS), f32),
            jax.ShapeDtypeStruct((8, 128), f32),
        ),
        in_specs=[any_, any_] + [vm] * 10,
        out_specs=(vm, vm, vm),
        scratch_shapes=[
            pltpu.VMEM((3, 4, 128, 384), f32),
            pltpu.VMEM((3, 2, 16, 256), f32),
            pltpu.VMEM((2, 1536, 768), jnp.bfloat16),
            pltpu.VMEM((32, 8, ENDS), f32),
            pltpu.VMEM((32, 8, ENDS), f32),
            pltpu.VMEM((DEVICES, ENDS), jnp.bfloat16),
            pltpu.VMEM((ENDS, DEVICES), jnp.bfloat16),
            pltpu.VMEM((2, DEVICES, 1, 128), f32),
            pltpu.VMEM((2, DEVICES, 1, 128), f32),
            dma, dma((3,)), dma, dma((3,)), dma((2,)), dma((2,)), dma((2,)),
        ],
        compiler_params=pltpu.CompilerParams(collective_id=9, has_side_effects=True, vmem_limit_bytes=VMEM_CAP),
        name="transient_steps",
    )(inverses, v0_send, hist, zero_in, ht, g, mmap, send_rank, send_dev, recv_rank, recv_dev, over)


def body(
    inverses, node_counts, sources, port_slot, end_slot, modal_map, delay_steps, wave_buffer, yc_decay, yc_residue,
    yc_direct, yc_state, prop_decay, prop_residue, prop_state,
):
    i, z = place()
    f32 = jnp.float32
    port_flat = port_slot.reshape(-1)
    end_flat = end_slot.reshape(-1)

    sub = jnp.arange(32, dtype=jnp.int32)[:, None]
    port = z * 8 + jnp.arange(8, dtype=jnp.int32)[None, :]
    code = ((i * 8 + sub // 4) * ENDS + (sub % 4) * 64 + port).astype(f32).reshape(-1)
    codes = jnp.zeros((1024,), f32).at[port_flat].set(code)
    codes = jnp.pad(codes.reshape(DEVICES, 1, 8), ((0, 0), (0, 0), (0, 120)))
    codes = swap(swap_all_kernel, codes, 1, "owner_codes")
    end_code = codes[:, 0, :8].reshape(-1)[end_flat].reshape(2, 128)

    hist0, zero_in, ht, g = line_responses(
        yc_decay, yc_residue, yc_direct, yc_state, prop_decay, prop_residue, prop_state, delay_steps, wave_buffer
    )
    shared = jnp.concatenate([ht.reshape(96, 128), g.reshape(96, 128), modal_map.reshape(36, 128)], axis=0)
    table = jnp.concatenate(
        [
            hist0.reshape(2, 96, 128), zero_in.reshape(2, 96, 128),
            jnp.broadcast_to(shared[None], (2, 228, 128)), end_code[::-1][:, None, :],
            jnp.zeros((2, 512 - 421, 128), f32),
        ],
        axis=1,
    )
    table = table.transpose(0, 2, 1).reshape(ENDS, 512)
    holder = jnp.zeros((1024,), jnp.int32).at[end_flat].set(jnp.arange(ENDS, dtype=jnp.int32))
    moved = swap(swap_all_kernel, table[holder].reshape(DEVICES, 8, 512), 2, "tables_to_ports")
    at_ports = moved.reshape(1024, 512)[port_flat].reshape(8, 32, 512)
    at_owner = swap(swap_line_kernel, at_ports, 3, "tables_to_owners")
    mine = at_owner.reshape(8, 4, 8, 512).transpose(3, 1, 0, 2).reshape(512, ENDS)

    def padded(part):
        return jnp.pad(part.reshape(-1, 6, ENDS), ((0, 0), (0, 2), (0, 0)))

    hist_t, zero_t, ht_t, g_t, map_t = (
        padded(mine[0:96]), padded(mine[96:192]), padded(mine[192:288]), padded(mine[288:384]), padded(mine[384:420])
    )
    partner = mine[420].astype(jnp.int32)
    dev, pos = partner // ENDS, partner % ENDS
    same = dev[:, None] == dev[None, :]
    own = jnp.arange(ENDS, dtype=jnp.int32)
    send_rank = jnp.sum((same & (own[:, None] < own[None, :])).astype(jnp.int32), axis=0)
    recv_rank = jnp.sum((same & (pos[:, None] < pos[None, :])).astype(jnp.int32), axis=0)
    over = jnp.full((8, 128), jnp.max(send_rank) >= SLOTS).astype(f32)

    still = jnp.einsum("src,nsc->nsr", inverses, sources, precision=lax.Precision.HIGH)
    v0_send = still.reshape(16, 8, 2, 2, 2, 64).transpose(1, 2, 0, 4, 3, 5).reshape(8, 2, 16, 256)

    inject, current, flag = run_steps(
        inverses, v0_send, hist_t, zero_t, ht_t, g_t, map_t, send_rank[None, :], dev[None, :], recv_rank[:, None],
        dev[:, None], over,
    )

    def quick(_):
        ports = lax.all_gather(inject, "line", axis=0)
        ports = ports.reshape(8, 2, 16, 6, 2, 64).transpose(2, 0, 1, 4, 3, 5).reshape(16, 32, 384)
        volts = still + jnp.einsum("src,nsc->nsr", inverses[:, :, :384], ports, precision=lax.Precision.HIGH)
        row_ids = z * 128 + jnp.arange(128, dtype=jnp.int32)
        volts = jnp.where((row_ids[None, :] < node_counts[:, None])[None], volts, 0.0)
        back = current[:, :6].reshape(96, 4, 8, 8).transpose(2, 1, 3, 0).reshape(8, 32, 96)
        back = swap(swap_line_kernel, jnp.pad(back, ((0, 0), (0, 0), (0, 32))), 4, "currents_to_ports")
        source_port = jnp.zeros((1024,), jnp.int32).at[port_flat].set(jnp.arange(ENDS, dtype=jnp.int32))
        back = back.reshape(ENDS, 128)[source_port].reshape(DEVICES, 8, 128)
        back = swap(swap_all_kernel, back, 5, "currents_to_lines")
        lines = back.reshape(1024, 128)[end_flat][:, :96].reshape(2, 128, 16, 6)
        return volts, lines.transpose(2, 0, 3, 1)

    def general(_):
        return general_body(
            inverses, node_counts, sources, port_slot, end_slot, modal_map, delay_steps, wave_buffer, yc_decay,
            yc_residue, yc_direct, yc_state, prop_decay, prop_residue, prop_state,
        )

    return lax.cond(flag[0, 0] > 0.0, general, quick, 0)


def read_delayed(extended, delay_steps, step_index, buffer_len):
    read_at = buffer_len + step_index - delay_steps
    depth = jnp.arange(extended.shape[2], dtype=jnp.int32)
    picker = (depth[None, :, None] == read_at[:, None, :]).astype(extended.dtype)
    return jnp.sum(extended * picker[None], axis=2)


def move_back(outgoing):
    returned = lax.all_to_all(outgoing, ("net", "line"), split_axis=1, concat_axis=1, tiled=True)
    return returned


def move_forward(sending):
    arrived = lax.all_to_all(sending, ("net", "line"), split_axis=1, concat_axis=1, tiled=True)
    return arrived


def general_body(
    inverses,
    node_counts,
    sources,
    port_slot,
    end_slot,
    modal_map,
    delay_steps,
    wave_buffer,
    yc_decay,
    yc_residue,
    yc_direct,
    yc_state,
    prop_decay,
    prop_residue,
    prop_state,
):
    net_size = lax.axis_size("net")
    line_size = lax.axis_size("line")
    device_count = net_size * line_size
    sub_count, row_count, node_total = inverses.shape
    step_count = sources.shape[0]
    port_cols = port_slot.shape[1]
    mode_count = modal_map.shape[0]
    line_count = end_slot.shape[1]
    buffer_len = wave_buffer.shape[2]
    port_total = port_cols * line_size
    slot_cap = max(2, 4 * sub_count * port_cols // device_count)
    slot_width = device_count * slot_cap
    line_pos = lax.axis_index("line")
    row_ids = line_pos * row_count + jnp.arange(row_count, dtype=jnp.int32)
    live_mask = row_ids[None, :] < node_counts[:, None]
    port_flat = port_slot.reshape(-1)
    end_flat = end_slot.reshape(-1)
    used_nodes = port_total * mode_count
    first_port = line_pos * port_cols
    extended = jnp.concatenate(
        [wave_buffer, jnp.zeros((2, mode_count, step_count, line_count), jnp.float32)], axis=2
    )
    volts_init = jnp.zeros((step_count, sub_count, row_count), jnp.float32)
    currents_init = jnp.zeros((step_count, 2, mode_count, line_count), jnp.float32)

    def advance(step_index, carried):
        yc_now, prop_now, extended, volts_acc, currents_acc = carried
        delayed = read_delayed(extended, delay_steps, step_index, buffer_len)
        prop_now = prop_decay[None] * prop_now + prop_residue[None] * delayed[::-1][:, :, None, :]
        history = jnp.sum(prop_now, axis=2)
        history_phase = jnp.sum(modal_map[None] * history[:, None], axis=2)
        outgoing = (
            jnp.zeros((mode_count, slot_width), jnp.float32)
            .at[:, end_flat]
            .set(history_phase.transpose(1, 0, 2).reshape(mode_count, 2 * line_count))
        )
        returned = move_back(outgoing)
        own_ports = (
            returned[:, port_flat]
            .reshape(mode_count, sub_count, port_cols)
            .transpose(1, 2, 0)
            .reshape(sub_count, port_cols * mode_count)
        )
        port_currents = lax.all_gather(own_ports, "line", axis=1, tiled=True)
        port_currents = (
            port_currents.reshape(sub_count, port_total, mode_count)
            .transpose(0, 2, 1)
            .reshape(sub_count, used_nodes)
        )
        source_now = lax.dynamic_index_in_dim(sources, step_index, 0, keepdims=False)
        injection = source_now + jnp.pad(port_currents, ((0, 0), (0, node_total - used_nodes)))
        solved = jnp.einsum("src,sc->sr", inverses, injection, precision=lax.Precision.HIGHEST)
        solved = jnp.where(live_mask, solved, 0.0)
        gathered = lax.all_gather(solved, "line", axis=1, tiled=True)
        by_mode = gathered[:, :used_nodes].reshape(sub_count, mode_count, port_total)
        own_volts = lax.dynamic_slice_in_dim(by_mode, first_port, port_cols, 2)
        own_volts = own_volts.transpose(1, 0, 2).reshape(mode_count, sub_count * port_cols)
        sending = jnp.zeros((mode_count, slot_width), jnp.float32).at[:, port_flat].set(own_volts)
        arrived = move_forward(sending)
        end_volts = arrived[:, end_flat].reshape(mode_count, 2, line_count)
        modal_volts = jnp.sum(modal_map[:, :, None, :] * end_volts[:, None], axis=0).transpose(
            1, 0, 2
        )
        yc_now = yc_decay[None] * yc_now + yc_residue[None] * modal_volts[:, :, None, :]
        charac = yc_direct[None] * modal_volts + jnp.sum(yc_now, axis=2)
        current = charac - history
        wave_out = 2.0 * charac - history
        extended = lax.dynamic_update_slice_in_dim(
            extended, wave_out[:, :, None, :], buffer_len + step_index, 2
        )
        volts_acc = lax.dynamic_update_slice_in_dim(volts_acc, solved[None], step_index, 0)
        currents_acc = lax.dynamic_update_slice_in_dim(currents_acc, current[None], step_index, 0)
        return (yc_now, prop_now, extended, volts_acc, currents_acc)

    final = lax.fori_loop(
        0, step_count, advance, (yc_state, prop_state, extended, volts_init, currents_init)
    )
    return (final[3], final[4])


def solution(mesh):
    placed = (
        P("net", "line", None),
        P("net"),
        P(None, "net", None),
        P("net", "line"),
        P(None, ("net", "line")),
        P(None, None, ("net", "line")),
        P(None, ("net", "line")),
        P(None, None, None, ("net", "line")),
        P(None, None, ("net", "line")),
        P(None, None, ("net", "line")),
        P(None, ("net", "line")),
        P(None, None, None, ("net", "line")),
        P(None, None, ("net", "line")),
        P(None, None, ("net", "line")),
        P(None, None, None, ("net", "line")),
    )
    return jax.shard_map(
        body,
        mesh=mesh,
        in_specs=placed,
        out_specs=(P(None, "net", "line"), P(None, None, None, ("net", "line"))),
        check_vma=False,
    )
```

```python
import jax
import jax.numpy as jnp
from jax import lax
from jax.experimental import pallas as pl
from jax.experimental.pallas import tpu as pltpu
from jax.sharding import PartitionSpec as P

MESH = pl.DeviceIdType.MESH
VMEM_CAP = 58 * 1024 * 1024
DEVICES = 128
SLOTS = 16
ENDS = 256
STEPS = 16
F32 = jnp.float32
BF16 = jnp.bfloat16
RING = (0, 1, 2, 1)
OFFSETS = sorted(
    [(a, b, c, e) for a in range(4) for b in range(4) for c in range(4) for e in range(2) if (a, b, c, e) != (0, 0, 0, 0)],
    key=lambda o: -(RING[o[0]] + RING[o[1]] + RING[o[2]] + 2 * o[3]),
)


def peer(i, z, offset):
    dy, dx, dz, dc = offset
    y, x, zz, c = i // 4, lax.rem(i, 4), z // 2, lax.rem(z, 2)
    ni = lax.rem(y + dy, 4) * 4 + lax.rem(x + dx, 4)
    nz = lax.rem(zz + dz, 4) * 2 + lax.rem(c + dc, 2)
    return ni, nz


def drain(ref, sem):
    pltpu.make_async_copy(ref, ref, sem).wait()


def split(value):
    high = value.astype(BF16)
    low = (value - high.astype(F32)).astype(BF16)
    return high, low


def dot_nt(left, right):
    return lax.dot_general(left, right, (((1,), (1,)), ((), ())), preferred_element_type=F32)


def iota(shape, dim):
    return lax.broadcasted_iota(jnp.int32, shape, dim)


def hot(condition):
    return jnp.where(condition, 1.0, 0.0).astype(BF16)


def steps_kernel(
    inverses, sources, port_row, port_col, end_row, end_col, mmap_in, delay, waves, yd, yr, ydir, ys_in, pd, pr, ps_in,
    volts_out, lines_out, flag_out,
    yst, pst, yim, pim, hbuf, table, code_send, code_recv, table_send, table_recv, port_send, own_recv,
    chunk, fixed, still, v0_send, v0, block, solve, mmap, hacc, cacc, ht, g,
    to_peer, from_peer, to_line, from_line, wave_send, wave_recv, cur_send, cur_recv, inj,
    code_sems, table_sems, port_sems, chunk_sem, v0_sems, block_sems, own_sem, wave_sems, cur_sems, inj_sems,
):
    i = lax.axis_index("net")
    z = lax.axis_index("line")
    me = i * 8 + z
    lane = iota((1, 128), 1)
    barrier = pltpu.get_barrier_semaphore()
    for offset in OFFSETS:
        pl.semaphore_signal(barrier, inc=1, device_id=peer(i, z, offset), device_id_type=MESH)

    def send_all(src_of, dst, sends, recvs):
        for offset in OFFSETS:
            ni, nz = peer(i, z, offset)
            pltpu.make_async_remote_copy(
                src_ref=src_of(ni * 8 + nz), dst_ref=dst, send_sem=sends, recv_sem=recvs,
                device_id=(ni, nz), device_id_type=MESH,
            ).start()

    def chunk_copy(c, slot):
        return pltpu.make_async_copy(inverses.at[pl.ds(c * 4, 4)], chunk.at[slot], chunk_sem.at[slot])

    chunk_copy(0, 0).start()

    f = iota((1, ENDS), 1)
    owner_dev = (i * 8 + f // 32).astype(F32)
    owner_pos = (lax.rem(f // 8, 4) * 64 + z * 8 + lax.rem(f, 8)).astype(F32)
    code_row = iota((128, ENDS), 0)
    codes = jnp.where(
        lax.rem(code_row, 8) == lax.rem(port_row[...], 8),
        jnp.where(code_row < 8, owner_dev, jnp.where(code_row < 16, owner_pos, 0.0)), 0.0,
    ).astype(BF16)
    code_send[...] = dot_nt(hot(iota((DEVICES, ENDS), 0) == port_row[...] // 8), codes)[:, None, :]

    pl.semaphore_wait(barrier, len(OFFSETS))
    send_all(lambda d: code_send.at[d], code_recv.at[me], code_sems.at[0], code_sems.at[1])
    code_recv[me] = code_send[me]

    @pl.when(z < 3)
    def _blocks():
        for k in range(1, 8):
            nz = lax.rem(z + k, 8)
            pltpu.make_async_remote_copy(
                src_ref=inverses.at[pl.ds(nz * 4, 4), :, pl.ds(0, 384)], dst_ref=block.at[z],
                send_sem=block_sems.at[3], recv_sem=block_sems.at[z],
                device_id=(i, nz), device_id_type=MESH,
            ).start()
        pltpu.make_async_copy(inverses.at[pl.ds(z * 4, 4), :, pl.ds(0, 384)], block.at[z], own_sem.at[0]).start()

    table[...] = jnp.zeros(table.shape, F32)
    yst[...] = ys_in[...]
    pst[...] = ps_in[...]
    yim[...] = yr[...]
    pim[...] = pr[...]
    depth = iota((6, 64, 128), 1)

    def respond(n, carry):
        pick = depth == (64 + n - delay[...])[:, None, :]
        ydec, pdec, pres = yd[...], pd[...], pr[...]
        for e in range(2):
            seen = jnp.sum(jnp.where(pick, waves[1 - e], 0.0), axis=1)
            now = pdec * pst[e] + pres * seen[:, None, :]
            pst[e] = now
            table[n, 0:6, e * 128:(e + 1) * 128] = jnp.sum(now, axis=1)
            free = ydec * yst[e]
            yst[e] = free
            table[16 + n, 0:6, e * 128:(e + 1) * 128] = jnp.sum(free, axis=1)
        first = jnp.where(n == 0, 1.0, 0.0)
        pnow, ynow = pim[...], yim[...]
        hbuf[n] = jnp.sum(pnow, axis=1)
        gnow = jnp.sum(ynow, axis=1) + first * ydir[...]
        table[48 + n, 0:6, 0:128] = gnow
        table[48 + n, 0:6, 128:256] = gnow
        pim[...] = pnow * pdec
        yim[...] = ynow * ydec
        return carry

    lax.fori_loop(0, STEPS, respond, 0)
    lag = delay[...]
    for k in range(1, STEPS):
        total = jnp.zeros((6, 128), F32)
        for m in range(k):
            total = total + jnp.where(lag == k - m, hbuf[m], 0.0)
        table[32 + k, 0:6, 0:128] = total
        table[32 + k, 0:6, 128:256] = total
    for k in range(6):
        for j in range(6):
            m = k * 6 + j
            row = mmap_in[k, j:j + 1, :]
            table[m // 2, 6 + m % 2:7 + m % 2, 0:128] = row
            table[m // 2, 6 + m % 2:7 + m % 2, 128:256] = row

    drain(code_recv.at[pl.ds(0, DEVICES - 1)], code_sems.at[1])
    got = code_recv[...].reshape(DEVICES, 128).astype(BF16)
    found = jnp.dot(hot(iota((ENDS, DEVICES), 1) == end_col[...] // 8), got, preferred_element_type=F32)
    code_lane = iota((ENDS, 128), 1)
    found = jnp.where(
        (lax.rem(code_lane, 8) == lax.rem(end_col[...], 8)) & (code_lane < 16), found, 0.0
    ).astype(BF16)
    end_owner = dot_nt(hot(iota((8, 128), 1) // 8 == iota((8, 128), 0)), found)
    found_col = found.astype(F32)
    end_dev_col = jnp.sum(jnp.where(code_lane < 8, found_col, 0.0), axis=1, keepdims=True)
    end_pos_col = jnp.sum(jnp.where(code_lane >= 8, found_col, 0.0), axis=1, keepdims=True)
    partner = jnp.concatenate([end_owner[0:2, 128:], end_owner[0:2, :128]], axis=1)
    table[32, 0:2, :] = partner
    table[32, 2:3, :] = jnp.full((1, ENDS), me).astype(F32)
    table[32, 3:4, :] = f.astype(F32)

    high, low = split(table[...].reshape(512, ENDS))
    parts = jnp.concatenate([high, low], axis=0)

    def fill(c, carry):
        pick = hot(iota((256, ENDS), 0) + c * 256 == end_row[...])
        rows = dot_nt(pick, parts)
        table_send[pl.ds(c * 32, 32)] = (rows[:, :512] + rows[:, 512:]).reshape(32, 8, 512)
        return carry

    lax.fori_loop(0, 4, fill, 0)
    send_all(lambda d: table_send.at[d], table_recv.at[me], table_sems.at[0], table_sems.at[1])
    table_recv[me] = table_send[me]

    def solve_sources(c, carry):
        slot = lax.rem(c, 2)
        chunk_copy(c, slot).wait()

        @pl.when(c < 7)
        def _next():
            chunk_copy(c + 1, 1 - slot).start()

        def one(s, carry):
            a_high, a_low = split(chunk[slot, s])
            matrix = jnp.concatenate([a_high, a_low], axis=0)
            fixed[c * 4 + s] = matrix[:, :384]
            s_high, s_low = split(sources[c * 4 + s])
            both = dot_nt(jnp.concatenate([s_high, s_low], axis=0), matrix)
            both = both[:STEPS] + both[STEPS:]
            still[c * 4 + s] = both[:, :128] + both[:, 128:]
            return carry

        lax.fori_loop(0, 4, one, 0)
        for t in range(2):
            first, second = still[c * 4 + 2 * t], still[c * 4 + 2 * t + 1]
            v0_send[c, t, :, 0:128] = jnp.where(lane < 64, first, pltpu.roll(second, 64, 1))
            v0_send[c, t, :, 128:256] = jnp.where(lane < 64, pltpu.roll(first, 64, 1), second)

        @pl.when((z < 3) & (c != z))
        def _send():
            pltpu.make_async_remote_copy(
                src_ref=v0_send.at[c], dst_ref=v0.at[z], send_sem=v0_sems.at[3], recv_sem=v0_sems.at[z],
                device_id=(i, c), device_id_type=MESH,
            ).start()

        @pl.when((z < 3) & (c == z))
        def _keep():
            v0[z] = v0_send[c]

        return carry

    lax.fori_loop(0, 8, solve_sources, 0)

    drain(table_recv.at[pl.ds(0, DEVICES - 1)], table_sems.at[1])
    at_port = jnp.zeros((ENDS, 1024), F32)
    for c in range(4):
        high, low = split(table_recv[c * 32:(c + 1) * 32].reshape(256, 512))
        pick = hot(iota((ENDS, 256), 1) + c * 256 == port_col[...])
        at_port = at_port + jnp.dot(pick, jnp.concatenate([high, low], axis=1), preferred_element_type=F32)
    port_send[...] = (at_port[:, :512] + at_port[:, 512:]).reshape(8, 4, 8, 512)
    for k in range(1, 8):
        nz = lax.rem(z + k, 8)
        pltpu.make_async_remote_copy(
            src_ref=port_send.at[nz], dst_ref=own_recv.at[:, z], send_sem=port_sems.at[0], recv_sem=port_sems.at[1],
            device_id=(i, nz), device_id_type=MESH,
        ).start()
    own_recv[:, z] = port_send[z]
    drain(own_recv.at[:, pl.ds(0, 7)], port_sems.at[1])

    mine = own_recv[...].reshape(ENDS, 512)
    turned = mine.T.reshape(64, 8, ENDS)
    real = iota((1, 8, ENDS), 1) < 6
    hacc[...] = jnp.zeros(hacc.shape, F32)
    cacc[...] = jnp.zeros(cacc.shape, F32)
    hacc[0:STEPS] = jnp.where(real, turned[0:16], 0.0)
    cacc[0:STEPS] = jnp.where(real, turned[16:32], 0.0)
    ht[...] = jnp.where(real, turned[32:48], 0.0)
    g[...] = jnp.where(real, turned[48:64], 0.0)
    mmap[...] = jnp.zeros(mmap.shape, F32)
    for k in range(6):
        for j in range(6):
            m = k * 6 + j
            mmap[k, j:j + 1, :] = turned[m // 2, 6 + m % 2:7 + m % 2, :]

    def rank_row(dev_row, dev_col):
        before = (dev_row == dev_col) & (iota((ENDS, ENDS), 0) < iota((ENDS, ENDS), 1))
        return jnp.sum(jnp.where(before, 1.0, 0.0), axis=0, keepdims=True).astype(jnp.int32)

    def rank_col(dev_row, dev_col, pos_row, pos_col):
        before = (dev_row == dev_col) & (pos_row < pos_col)
        return jnp.sum(jnp.where(before, 1.0, 0.0), axis=1, keepdims=True).astype(jnp.int32)

    peer_row, peer_col = turned[32, 0:1], mine[:, 256:257]
    line_row, line_col = turned[32, 2:3], mine[:, 258:259]
    peer_rank = rank_row(peer_row, peer_col)
    line_rank = rank_row(line_row, line_col)
    peer_rank_in = rank_col(peer_row, peer_col, turned[32, 1:2], mine[:, 257:258])
    line_rank_in = rank_col(end_owner[0:1], end_dev_col, end_owner[1:2], end_pos_col)
    to_peer[...] = hot(iota((DEVICES, ENDS), 0) == peer_row.astype(jnp.int32))
    to_line[...] = hot(iota((DEVICES, ENDS), 0) == line_row.astype(jnp.int32))
    from_peer[...] = hot(iota((ENDS, DEVICES), 1) == peer_col.astype(jnp.int32))
    from_line[...] = hot(iota((ENDS, DEVICES), 1) == end_dev_col.astype(jnp.int32))
    worst_rank = jnp.maximum(
        jnp.max(peer_rank, axis=1, keepdims=True), jnp.max(line_rank, axis=1, keepdims=True)
    )
    over = jnp.where(worst_rank >= SLOTS, 1.0, 0.0)
    flag_lane = jnp.where(lane == 127, 1.0, 0.0) * over
    mode_pick = hot(lax.rem(iota((8, 256), 1), 128) // SLOTS == iota((8, 256), 0))

    for src_z in range(3):
        @pl.when(z != src_z)
        def _wait():
            drain(block.at[src_z], block_sems.at[src_z])
            drain(v0.at[src_z], v0_sems.at[src_z])

        @pl.when(z == src_z)
        def _own():
            drain(block.at[src_z], own_sem.at[0])

    def build(t, carry):
        for src_z in range(3):
            for h in range(2):
                for kk in range(2):
                    rows = block[src_z, t * 2 + h, kk * 64:(kk + 1) * 64, :]
                    row0 = (src_z * 2 + kk) * 128 + h * 64
                    for k in range(6):
                        tile = rows[:, (k // 2) * 128:(k // 2 + 1) * 128]
                        if k % 2 != h:
                            tile = pltpu.roll(tile, 64, 1)
                        tile = jnp.where((lane // 64) == h, tile, 0.0)
                        high, low = split(tile)
                        solve[t, row0:row0 + 64, k * 128:(k + 1) * 128] = high
                        solve[t, 768 + row0:768 + row0 + 64, k * 128:(k + 1) * 128] = low
        return carry

    lax.fori_loop(0, 2, build, 0)

    def to_rows(values, rank, onehot):
        spread = jnp.concatenate(
            [jnp.broadcast_to(values[j:j + 1], (SLOTS, ENDS)) for j in range(6)]
            + [jnp.zeros((2 * SLOTS, ENDS), F32)], axis=0
        )
        slot = lax.rem(iota((DEVICES, ENDS), 0), SLOTS)
        high, low = split(jnp.where(slot == rank, spread, 0.0))
        rows = dot_nt(onehot[...], jnp.concatenate([high, low], axis=0))
        return rows[:, :128] + rows[:, 128:]

    def from_rows(rows, rank, onehot):
        high, low = split(rows)
        found = jnp.dot(onehot[...], jnp.concatenate([high, low], axis=1), preferred_element_type=F32)
        slot = lax.rem(iota((ENDS, 256), 1), SLOTS)
        found = jnp.where(slot == rank, found, 0.0).astype(BF16)
        return dot_nt(mode_pick, found)

    def take_currents(n):
        drain(cur_recv.at[n, pl.ds(0, DEVICES - 1)], cur_sems.at[n])
        lines_out[n] = from_rows(cur_recv[n].reshape(DEVICES, 128), line_rank_in, from_line)

    def step(n, carry):
        delayed, worst = carry
        hist = hacc[n] + ht[1] * delayed
        phase = [jnp.sum(mmap[k] * hist, axis=0, keepdims=True) for k in range(6)]
        volts = []
        pieces = []
        for t in range(2):
            rows = [p[:, t * 128:(t + 1) * 128] for p in phase]
            pieces += rows
            high, low = split(jnp.concatenate(rows, axis=1))
            both = dot_nt(jnp.concatenate([high, low], axis=0), solve[t])
            total = jnp.sum(both, axis=0, keepdims=True)
            total = total[:, :768] + total[:, 768:]
            base = jnp.concatenate([v0[a, t, pl.ds(n, 1), :] for a in range(3)], axis=1)
            volts.append(total + base)
        inj[z, n, 0:12] = jnp.concatenate(pieces, axis=0)
        modal = jnp.zeros((8, ENDS), F32)
        for k in range(6):
            row = jnp.concatenate([v[:, k * 128:(k + 1) * 128] for v in volts], axis=1)
            modal = modal + mmap[k] * row
        charac = cacc[n] + g[0] * modal
        wave = 2.0 * charac - hist

        @pl.when(n < STEPS - 1)
        def _waves():
            wave_send[n] = (to_rows(wave, peer_rank, to_peer) + flag_lane)[:, None, :]
            send_all(lambda d: wave_send.at[n, d], wave_recv.at[n, me], wave_sems.at[0, n], wave_sems.at[1, n])
            wave_recv[n, me] = wave_send[n, me]

        cur_send[n] = to_rows(charac - hist, line_rank, to_line)[:, None, :]
        send_all(lambda d: cur_send.at[n, d], cur_recv.at[n, me], cur_sems.at[STEPS + n], cur_sems.at[n])
        cur_recv[n, me] = cur_send[n, me]
        for k in range(1, 8):
            nz = lax.rem(z + k, 8)
            pltpu.make_async_remote_copy(
                src_ref=inj.at[z, n], dst_ref=inj.at[z, n], send_sem=inj_sems.at[0], recv_sem=inj_sems.at[1],
                device_id=(i, nz), device_id_type=MESH,
            ).start()

        for k in range(2, STEPS):
            hacc[n + k - 1] = hacc[n + k - 1] + ht[k] * delayed
        for k in range(1, STEPS):
            cacc[n + k] = cacc[n + k] + g[k] * modal

        @pl.when(n > 0)
        def _lines():
            take_currents(n - 1)

        last = jnp.minimum(n, STEPS - 2)

        @pl.when(n < STEPS - 1)
        def _arrive():
            drain(wave_recv.at[n, pl.ds(0, DEVICES - 1)], wave_sems.at[1, n])

        rows = wave_recv[last].reshape(DEVICES, 128)
        worst = jnp.maximum(worst, jnp.max(rows[:, 127:128], axis=0, keepdims=True))
        return from_rows(rows, peer_rank_in, from_peer), worst

    delayed, worst = lax.fori_loop(0, STEPS, step, (jnp.zeros((8, ENDS), F32), jnp.zeros((1, 1), F32)))
    flag_out[...] = jnp.broadcast_to(worst, flag_out.shape)

    drain(inj.at[pl.ds(0, 7)], inj_sems.at[1])

    def finish(a, carry):
        for t in range(2):
            tiles = [inj[a, :, t * 6 + k, :] for k in range(6)]
            for h in range(2):
                s = a * 4 + t * 2 + h
                left = []
                for u in range(3):
                    even, odd = tiles[2 * u], tiles[2 * u + 1]
                    if h == 0:
                        left.append(jnp.where(lane < 64, even, pltpu.roll(odd, 64, 1)))
                    else:
                        left.append(jnp.where(lane < 64, pltpu.roll(even, 64, 1), odd))
                high, low = split(jnp.concatenate(left, axis=1))
                both = dot_nt(jnp.concatenate([high, low], axis=0), fixed[s])
                both = both[:STEPS] + both[STEPS:]
                volts_out[s] = still[s] + both[:, :128] + both[:, 128:]
        return carry

    lax.fori_loop(0, 8, finish, 0)
    take_currents(STEPS - 1)

    drain(code_send.at[pl.ds(0, DEVICES - 1)], code_sems.at[0])
    drain(table_send.at[pl.ds(0, DEVICES - 1)], table_sems.at[0])
    drain(port_send.at[pl.ds(0, 7)], port_sems.at[0])
    drain(inj.at[pl.ds(0, 7)], inj_sems.at[0])

    def sent(n, carry):
        drain(cur_send.at[n, pl.ds(0, DEVICES - 1)], cur_sems.at[STEPS + n])

        @pl.when(n < STEPS - 1)
        def _wave():
            drain(wave_send.at[n, pl.ds(0, DEVICES - 1)], wave_sems.at[0, n])
        return carry

    lax.fori_loop(0, STEPS, sent, 0)

    @pl.when(z < 3)
    def _sent():
        drain(v0_send.at[pl.ds(0, 7)], v0_sems.at[3])
        drain(inverses.at[pl.ds(0, 28), :, pl.ds(0, 384)], block_sems.at[3])


def run_steps(*operands):
    vm = pl.BlockSpec(memory_space=pltpu.VMEM)
    dma = pltpu.SemaphoreType.DMA
    rows = (STEPS, DEVICES, 1, 128)
    return pl.pallas_call(
        steps_kernel,
        out_shape=(
            jax.ShapeDtypeStruct((32, STEPS, 128), F32),
            jax.ShapeDtypeStruct((STEPS, 8, ENDS), F32),
            jax.ShapeDtypeStruct((8, 128), F32),
        ),
        in_specs=[pl.BlockSpec(memory_space=pl.ANY)] + [vm] * (len(operands) - 1),
        out_specs=(vm, vm, vm),
        scratch_shapes=[
            pltpu.VMEM((2, 6, 30, 128), F32),
            pltpu.VMEM((2, 6, 30, 128), F32),
            pltpu.VMEM((6, 30, 128), F32),
            pltpu.VMEM((6, 30, 128), F32),
            pltpu.VMEM((STEPS, 6, 128), F32),
            pltpu.VMEM((64, 8, ENDS), F32),
            pltpu.VMEM((DEVICES, 1, 128), F32),
            pltpu.VMEM((DEVICES, 1, 128), F32),
            pltpu.VMEM((DEVICES, 8, 512), F32),
            pltpu.VMEM((DEVICES, 8, 512), F32),
            pltpu.VMEM((8, 4, 8, 512), F32),
            pltpu.VMEM((4, 8, 8, 512), F32),
            pltpu.VMEM((2, 4, 128, 1024), F32),
            pltpu.VMEM((32, 256, 384), BF16),
            pltpu.VMEM((32, STEPS, 128), F32),
            pltpu.VMEM((8, 2, STEPS, 256), F32),
            pltpu.VMEM((3, 2, STEPS, 256), F32),
            pltpu.VMEM((3, 4, 128, 384), F32),
            pltpu.VMEM((2, 1536, 768), BF16),
            pltpu.VMEM((6, 8, ENDS), F32),
            pltpu.VMEM((32, 8, ENDS), F32),
            pltpu.VMEM((32, 8, ENDS), F32),
            pltpu.VMEM((STEPS, 8, ENDS), F32),
            pltpu.VMEM((STEPS, 8, ENDS), F32),
            pltpu.VMEM((DEVICES, ENDS), BF16),
            pltpu.VMEM((ENDS, DEVICES), BF16),
            pltpu.VMEM((DEVICES, ENDS), BF16),
            pltpu.VMEM((ENDS, DEVICES), BF16),
            pltpu.VMEM(rows, F32),
            pltpu.VMEM(rows, F32),
            pltpu.VMEM(rows, F32),
            pltpu.VMEM(rows, F32),
            pltpu.VMEM((8, STEPS, 16, 128), F32),
            dma((2,)), dma((2,)), dma((2,)), dma((2,)), dma((4,)), dma((4,)), dma((1,)), dma((2, STEPS)),
            dma((2 * STEPS,)), dma((2,)),
        ],
        compiler_params=pltpu.CompilerParams(collective_id=0, has_side_effects=True, vmem_limit_bytes=VMEM_CAP),
        name="transient_steps",
    )(*operands)


def body(
    inverses, node_counts, sources, port_slot, end_slot, modal_map, delay_steps, wave_buffer, yc_decay, yc_residue,
    yc_direct, yc_state, prop_decay, prop_residue, prop_state,
):
    z = lax.axis_index("line")
    port_flat = port_slot.reshape(-1)
    end_flat = end_slot.reshape(-1)
    volts, lines, flag = run_steps(
        inverses, sources.transpose(1, 0, 2), port_flat[None, :], port_flat[:, None], end_flat[None, :],
        end_flat[:, None], modal_map, delay_steps, wave_buffer, yc_decay, yc_residue, yc_direct, yc_state,
        prop_decay, prop_residue, prop_state,
    )

    def quick(_):
        row_ids = z * 128 + jnp.arange(128, dtype=jnp.int32)
        live = row_ids[None, :] < node_counts[:, None]
        ends = lines[:, :6].reshape(STEPS, 6, 2, 128)
        return jnp.where(live[None], volts.transpose(1, 0, 2), 0.0), ends.transpose(0, 2, 1, 3)

    def general(_):
        return general_body(
            inverses, node_counts, sources, port_slot, end_slot, modal_map, delay_steps, wave_buffer, yc_decay,
            yc_residue, yc_direct, yc_state, prop_decay, prop_residue, prop_state,
        )

    return lax.cond(flag[0, 0] > 0.0, general, quick, 0)


def read_delayed(extended, delay_steps, step_index, buffer_len):
    read_at = buffer_len + step_index - delay_steps
    depth = jnp.arange(extended.shape[2], dtype=jnp.int32)
    picker = (depth[None, :, None] == read_at[:, None, :]).astype(extended.dtype)
    return jnp.sum(extended * picker[None], axis=2)


def move_back(outgoing):
    returned = lax.all_to_all(outgoing, ("net", "line"), split_axis=1, concat_axis=1, tiled=True)
    return returned


def move_forward(sending):
    arrived = lax.all_to_all(sending, ("net", "line"), split_axis=1, concat_axis=1, tiled=True)
    return arrived


def general_body(
    inverses,
    node_counts,
    sources,
    port_slot,
    end_slot,
    modal_map,
    delay_steps,
    wave_buffer,
    yc_decay,
    yc_residue,
    yc_direct,
    yc_state,
    prop_decay,
    prop_residue,
    prop_state,
):
    net_size = lax.axis_size("net")
    line_size = lax.axis_size("line")
    device_count = net_size * line_size
    sub_count, row_count, node_total = inverses.shape
    step_count = sources.shape[0]
    port_cols = port_slot.shape[1]
    mode_count = modal_map.shape[0]
    line_count = end_slot.shape[1]
    buffer_len = wave_buffer.shape[2]
    port_total = port_cols * line_size
    slot_cap = max(2, 4 * sub_count * port_cols // device_count)
    slot_width = device_count * slot_cap
    line_pos = lax.axis_index("line")
    row_ids = line_pos * row_count + jnp.arange(row_count, dtype=jnp.int32)
    live_mask = row_ids[None, :] < node_counts[:, None]
    port_flat = port_slot.reshape(-1)
    end_flat = end_slot.reshape(-1)
    used_nodes = port_total * mode_count
    first_port = line_pos * port_cols
    extended = jnp.concatenate(
        [wave_buffer, jnp.zeros((2, mode_count, step_count, line_count), jnp.float32)], axis=2
    )
    volts_init = jnp.zeros((step_count, sub_count, row_count), jnp.float32)
    currents_init = jnp.zeros((step_count, 2, mode_count, line_count), jnp.float32)

    def advance(step_index, carried):
        yc_now, prop_now, extended, volts_acc, currents_acc = carried
        delayed = read_delayed(extended, delay_steps, step_index, buffer_len)
        prop_now = prop_decay[None] * prop_now + prop_residue[None] * delayed[::-1][:, :, None, :]
        history = jnp.sum(prop_now, axis=2)
        history_phase = jnp.sum(modal_map[None] * history[:, None], axis=2)
        outgoing = (
            jnp.zeros((mode_count, slot_width), jnp.float32)
            .at[:, end_flat]
            .set(history_phase.transpose(1, 0, 2).reshape(mode_count, 2 * line_count))
        )
        returned = move_back(outgoing)
        own_ports = (
            returned[:, port_flat]
            .reshape(mode_count, sub_count, port_cols)
            .transpose(1, 2, 0)
            .reshape(sub_count, port_cols * mode_count)
        )
        port_currents = lax.all_gather(own_ports, "line", axis=1, tiled=True)
        port_currents = (
            port_currents.reshape(sub_count, port_total, mode_count)
            .transpose(0, 2, 1)
            .reshape(sub_count, used_nodes)
        )
        source_now = lax.dynamic_index_in_dim(sources, step_index, 0, keepdims=False)
        injection = source_now + jnp.pad(port_currents, ((0, 0), (0, node_total - used_nodes)))
        solved = jnp.einsum("src,sc->sr", inverses, injection, precision=lax.Precision.HIGHEST)
        solved = jnp.where(live_mask, solved, 0.0)
        gathered = lax.all_gather(solved, "line", axis=1, tiled=True)
        by_mode = gathered[:, :used_nodes].reshape(sub_count, mode_count, port_total)
        own_volts = lax.dynamic_slice_in_dim(by_mode, first_port, port_cols, 2)
        own_volts = own_volts.transpose(1, 0, 2).reshape(mode_count, sub_count * port_cols)
        sending = jnp.zeros((mode_count, slot_width), jnp.float32).at[:, port_flat].set(own_volts)
        arrived = move_forward(sending)
        end_volts = arrived[:, end_flat].reshape(mode_count, 2, line_count)
        modal_volts = jnp.sum(modal_map[:, :, None, :] * end_volts[:, None], axis=0).transpose(
            1, 0, 2
        )
        yc_now = yc_decay[None] * yc_now + yc_residue[None] * modal_volts[:, :, None, :]
        charac = yc_direct[None] * modal_volts + jnp.sum(yc_now, axis=2)
        current = charac - history
        wave_out = 2.0 * charac - history
        extended = lax.dynamic_update_slice_in_dim(
            extended, wave_out[:, :, None, :], buffer_len + step_index, 2
        )
        volts_acc = lax.dynamic_update_slice_in_dim(volts_acc, solved[None], step_index, 0)
        currents_acc = lax.dynamic_update_slice_in_dim(currents_acc, current[None], step_index, 0)
        return (yc_now, prop_now, extended, volts_acc, currents_acc)

    final = lax.fori_loop(
        0, step_count, advance, (yc_state, prop_state, extended, volts_init, currents_init)
    )
    return (final[3], final[4])


def solution(mesh):
    placed = (
        P("net", "line", None),
        P("net"),
        P(None, "net", None),
        P("net", "line"),
        P(None, ("net", "line")),
        P(None, None, ("net", "line")),
        P(None, ("net", "line")),
        P(None, None, None, ("net", "line")),
        P(None, None, ("net", "line")),
        P(None, None, ("net", "line")),
        P(None, ("net", "line")),
        P(None, None, None, ("net", "line")),
        P(None, None, ("net", "line")),
        P(None, None, ("net", "line")),
        P(None, None, None, ("net", "line")),
    )
    return jax.shard_map(
        body,
        mesh=mesh,
        in_specs=placed,
        out_specs=(P(None, "net", "line"), P(None, None, None, ("net", "line"))),
        check_vma=False,
    )
```

```python
import jax
import jax.numpy as jnp
from jax import lax
from jax.experimental import pallas as pl
from jax.experimental.pallas import tpu as pltpu
from jax.sharding import PartitionSpec as P

MESH = pl.DeviceIdType.MESH
VMEM_CAP = 58 * 1024 * 1024
DEVICES = 128
SLOTS = 16
ENDS = 256
STEPS = 16
F32 = jnp.float32
BF16 = jnp.bfloat16
RING = (0, 1, 2, 1)
OFFSETS = sorted(
    [(a, b, c, e) for a in range(4) for b in range(4) for c in range(4) for e in range(2) if (a, b, c, e) != (0, 0, 0, 0)],
    key=lambda o: -(RING[o[0]] + RING[o[1]] + RING[o[2]] + 2 * o[3]),
)


def peer(i, z, offset):
    dy, dx, dz, dc = offset
    y, x, zz, c = i // 4, lax.rem(i, 4), z // 2, lax.rem(z, 2)
    ni = lax.rem(y + dy, 4) * 4 + lax.rem(x + dx, 4)
    nz = lax.rem(zz + dz, 4) * 2 + lax.rem(c + dc, 2)
    return ni, nz


def drain(ref, sem):
    pltpu.make_async_copy(ref, ref, sem).wait()


def split(value):
    high = value.astype(BF16)
    low = (value - high.astype(F32)).astype(BF16)
    return high, low


def dot_nt(left, right):
    return lax.dot_general(left, right, (((1,), (1,)), ((), ())), preferred_element_type=F32)


def iota(shape, dim):
    return lax.broadcasted_iota(jnp.int32, shape, dim)


def hot(condition):
    return jnp.where(condition, 1.0, 0.0).astype(BF16)


def steps_kernel(
    inverses, counts, sources, port_row, end_row, mmap_in, delay, waves, yd, yr, ydir, ys_in, pd, pr, ps_in,
    volts_out, lines_out, flag_out,
    yst, pst, yim, pim, hbuf, table, code_send, code_recv, table_send, table_recv, port_send, own_recv,
    chunk, fixed, still, v0, block, relay, solve, mmap, hacc, cacc, ht, g,
    to_peer, from_peer, to_line, from_line, wave_send, wave_recv, cur_send, cur_recv, inj,
    code_sems, table_sems, port_sems, chunk_sem, v0_sems, block_sems, relay_sems, own_sem, wave_sems, cur_sems, inj_sems,
):
    i = lax.axis_index("net")
    z = lax.axis_index("line")
    me = i * 8 + z
    lane = iota((1, 128), 1)
    barrier = pltpu.get_barrier_semaphore()
    for offset in OFFSETS:
        pl.semaphore_signal(barrier, inc=1, device_id=peer(i, z, offset), device_id_type=MESH)

    def send_all(src_of, dst, sends, recvs):
        for offset in OFFSETS:
            ni, nz = peer(i, z, offset)
            pltpu.make_async_remote_copy(
                src_ref=src_of(ni * 8 + nz), dst_ref=dst, send_sem=sends, recv_sem=recvs,
                device_id=(ni, nz), device_id_type=MESH,
            ).start()

    def chunk_copy(c, slot):
        return pltpu.make_async_copy(inverses.at[pl.ds(c * 4, 4)], chunk.at[slot], chunk_sem.at[slot])

    chunk_copy(0, 0).start()

    def column(row):
        return jnp.broadcast_to(row.astype(F32), (128, ENDS)).T[:, 0:1].astype(jnp.int32)

    port_col = column(port_row[...])
    end_col = column(end_row[...])

    f = iota((1, ENDS), 1)
    owner_dev = (i * 8 + f // 32).astype(F32)
    owner_pos = (lax.rem(f // 8, 4) * 64 + z * 8 + lax.rem(f, 8)).astype(F32)
    code_row = iota((128, ENDS), 0)
    codes = jnp.where(
        lax.rem(code_row, 8) == lax.rem(port_row[...], 8),
        jnp.where(code_row < 8, owner_dev, jnp.where(code_row < 16, owner_pos, 0.0)), 0.0,
    ).astype(BF16)
    code_send[...] = dot_nt(hot(iota((DEVICES, ENDS), 0) == port_row[...] // 8), codes)[:, None, :]

    pl.semaphore_wait(barrier, len(OFFSETS))
    send_all(lambda d: code_send.at[d], code_recv.at[me], code_sems.at[0], code_sems.at[1])
    code_recv[me] = code_send[me]

    chip, core = z // 2, lax.rem(z, 2)

    def block_piece(dz, dc, first, count):
        nz = lax.rem(chip + dz, 4) * 2 + lax.rem(core + dc, 2)
        pltpu.make_async_remote_copy(
            src_ref=inverses.at[pl.ds(nz * 4 + first, count), :, pl.ds(0, 384)],
            dst_ref=block.at[z, pl.ds(first, count)], send_sem=block_sems.at[3], recv_sem=block_sems.at[z],
            device_id=(i, nz), device_id_type=MESH,
        ).start()

    @pl.when(z < 2)
    def _two_hops():
        for dc in range(2):
            nz = 4 + lax.rem(core + dc, 2)
            pltpu.make_async_remote_copy(
                src_ref=inverses.at[pl.ds(nz * 4 + 2, 2), :, pl.ds(0, 384)], dst_ref=relay.at[pl.ds(z * 2, 2)],
                send_sem=block_sems.at[3], recv_sem=relay_sems.at[z],
                device_id=(i, nz + 2), device_id_type=MESH,
            ).start()
            block_piece(2, dc, 0, 2)

    @pl.when(z == 2)
    def _two_hops_whole():
        for dc in range(2):
            nz = 6 + dc
            pltpu.make_async_remote_copy(
                src_ref=inverses.at[pl.ds(nz * 4, 4), :, pl.ds(0, 384)], dst_ref=relay,
                send_sem=block_sems.at[3], recv_sem=relay_sems.at[0],
                device_id=(i, nz - 2), device_id_type=MESH,
            ).start()

    @pl.when(z < 3)
    def _own():
        pltpu.make_async_copy(inverses.at[pl.ds(z * 4, 4), :, pl.ds(0, 384)], block.at[z], own_sem.at[0]).start()

    table[...] = jnp.zeros(table.shape, F32)
    for e in range(2):
        yst[e] = ys_in[:, :, e, :]
        pst[e] = ps_in[:, :, e, :]
    yim[...] = yr[...]
    pim[...] = pr[...]
    depth = iota((6, 64, 128), 1)

    def respond(n, carry):
        pick = depth == (64 + n - delay[...])[:, None, :]
        ydec, pdec, pres = yd[...], pd[...], pr[...]
        for e in range(2):
            seen = jnp.sum(jnp.where(pick, waves[1 - e], 0.0), axis=1)
            now = pdec * pst[e] + pres * seen[:, None, :]
            pst[e] = now
            table[n, 0:6, e * 128:(e + 1) * 128] = jnp.sum(now, axis=1)
            free = ydec * yst[e]
            yst[e] = free
            table[16 + n, 0:6, e * 128:(e + 1) * 128] = jnp.sum(free, axis=1)
        first = jnp.where(n == 0, 1.0, 0.0)
        pnow, ynow = pim[...], yim[...]
        hbuf[n] = jnp.sum(pnow, axis=1)
        gnow = jnp.sum(ynow, axis=1) + first * ydir[...]
        table[48 + n, 0:6, 0:128] = gnow
        table[48 + n, 0:6, 128:256] = gnow
        pim[...] = pnow * pdec
        yim[...] = ynow * ydec
        return carry

    lax.fori_loop(0, STEPS, respond, 0)
    lag = delay[...]
    for k in range(1, STEPS):
        total = jnp.zeros((6, 128), F32)
        for m in range(k):
            total = total + jnp.where(lag == k - m, hbuf[m], 0.0)
        table[32 + k, 0:6, 0:128] = total
        table[32 + k, 0:6, 128:256] = total
    for k in range(6):
        for j in range(6):
            m = k * 6 + j
            row = mmap_in[k, j:j + 1, :]
            table[m // 2, 6 + m % 2:7 + m % 2, 0:128] = row
            table[m // 2, 6 + m % 2:7 + m % 2, 128:256] = row

    drain(code_recv.at[pl.ds(0, DEVICES - 1)], code_sems.at[1])
    got = code_recv[...].reshape(DEVICES, 128).astype(BF16)
    found = jnp.dot(hot(iota((ENDS, DEVICES), 1) == end_col // 8), got, preferred_element_type=F32)
    code_lane = iota((ENDS, 128), 1)
    found = jnp.where(
        (lax.rem(code_lane, 8) == lax.rem(end_col, 8)) & (code_lane < 16), found, 0.0
    ).astype(BF16)
    end_owner = dot_nt(hot(iota((8, 128), 1) // 8 == iota((8, 128), 0)), found)
    found_col = found.astype(F32)
    end_dev_col = jnp.sum(jnp.where(code_lane < 8, found_col, 0.0), axis=1, keepdims=True)
    end_pos_col = jnp.sum(jnp.where(code_lane >= 8, found_col, 0.0), axis=1, keepdims=True)
    partner = jnp.concatenate([end_owner[0:2, 128:], end_owner[0:2, :128]], axis=1)
    table[32, 0:2, :] = partner
    table[32, 2:3, :] = jnp.full((1, ENDS), me).astype(F32)
    table[32, 3:4, :] = f.astype(F32)

    high, low = split(table[...].reshape(512, ENDS))
    parts = jnp.concatenate([high, low], axis=0)

    def fill(c, carry):
        pick = hot(iota((256, ENDS), 0) + c * 256 == end_row[...])
        rows = dot_nt(pick, parts)
        table_send[pl.ds(c * 32, 32)] = (rows[:, :512] + rows[:, 512:]).reshape(32, 8, 512)
        return carry

    lax.fori_loop(0, 4, fill, 0)
    send_all(lambda d: table_send.at[d], table_recv.at[me], table_sems.at[0], table_sems.at[1])
    table_recv[me] = table_send[me]

    @pl.when(z < 3)
    def _second_part():
        block_piece(0, 1, 0, 4)
        block_piece(1, 0, 0, 1)
        block_piece(3, 0, 0, 1)

    def solve_sources(c, carry):
        slot = lax.rem(c, 2)
        chunk_copy(c, slot).wait()

        @pl.when(c < 7)
        def _next():
            chunk_copy(c + 1, 1 - slot).start()

        def one(s, carry):
            a_high, a_low = split(chunk[slot, s])
            matrix = jnp.concatenate([a_high, a_low], axis=0)
            fixed[c * 4 + s] = matrix[:, :384]
            s_high, s_low = split(sources[:, pl.ds(c * 4 + s, 1), :].reshape(STEPS, 1024))
            both = dot_nt(jnp.concatenate([s_high, s_low], axis=0), matrix)
            both = both[:STEPS] + both[STEPS:]
            still[c * 4 + s] = both[:, :128] + both[:, 128:]
            return carry

        lax.fori_loop(0, 4, one, 0)
        @pl.when((z < 3) & (c != z))
        def _send():
            pltpu.make_async_remote_copy(
                src_ref=still.at[pl.ds(c * 4, 4)], dst_ref=v0.at[z], send_sem=v0_sems.at[3], recv_sem=v0_sems.at[z],
                device_id=(i, c), device_id_type=MESH,
            ).start()

        @pl.when((z < 3) & (c == z))
        def _keep():
            v0[z] = still[pl.ds(c * 4, 4)]

        return carry

    lax.fori_loop(0, 8, solve_sources, 0)

    @pl.when(z >= 6)
    def _relay():
        for src_z in range(2):
            part = relay.at[pl.ds(src_z * 2, 2)]
            drain(part, relay_sems.at[src_z])
            pltpu.make_async_remote_copy(
                src_ref=part, dst_ref=block.at[src_z, pl.ds(2, 2)], send_sem=relay_sems.at[2],
                recv_sem=block_sems.at[src_z], device_id=(i, z - 2), device_id_type=MESH,
            ).start()

    @pl.when((z == 4) | (z == 5))
    def _relay_up():
        drain(relay, relay_sems.at[0])
        pltpu.make_async_remote_copy(
            src_ref=relay, dst_ref=block.at[2], send_sem=relay_sems.at[2], recv_sem=block_sems.at[2],
            device_id=(i, z + 2), device_id_type=MESH,
        ).start()

    drain(table_recv.at[pl.ds(0, DEVICES - 1)], table_sems.at[1])
    at_port = jnp.zeros((ENDS, 1024), F32)
    for c in range(4):
        high, low = split(table_recv[c * 32:(c + 1) * 32].reshape(256, 512))
        pick = hot(iota((ENDS, 256), 1) + c * 256 == port_col)
        at_port = at_port + jnp.dot(pick, jnp.concatenate([high, low], axis=1), preferred_element_type=F32)
    port_send[...] = (at_port[:, :512] + at_port[:, 512:]).reshape(8, 4, 8, 512)
    for k in range(1, 8):
        nz = lax.rem(z + k, 8)
        pltpu.make_async_remote_copy(
            src_ref=port_send.at[nz], dst_ref=own_recv.at[:, z], send_sem=port_sems.at[0], recv_sem=port_sems.at[1],
            device_id=(i, nz), device_id_type=MESH,
        ).start()
    own_recv[:, z] = port_send[z]

    @pl.when(z < 3)
    def _third_part():
        for first, count in ((1, 1), (2, 2)):
            block_piece(1, 0, first, count)
            block_piece(3, 0, first, count)
        for first in (0, 2):
            block_piece(1, 1, first, 2)
            block_piece(3, 1, first, 2)

    drain(own_recv.at[:, pl.ds(0, 7)], port_sems.at[1])

    mine = own_recv[...].reshape(ENDS, 512)
    turned = mine.T.reshape(64, 8, ENDS)
    real = iota((1, 8, ENDS), 1) < 6
    hacc[...] = jnp.zeros(hacc.shape, F32)
    cacc[...] = jnp.zeros(cacc.shape, F32)
    hacc[0:STEPS] = jnp.where(real, turned[0:16], 0.0)
    cacc[0:STEPS] = jnp.where(real, turned[16:32], 0.0)
    ht[...] = jnp.where(real, turned[32:48], 0.0)
    g[...] = jnp.where(real, turned[48:64], 0.0)
    mmap[...] = jnp.zeros(mmap.shape, F32)
    for k in range(6):
        for j in range(6):
            m = k * 6 + j
            mmap[k, j:j + 1, :] = turned[m // 2, 6 + m % 2:7 + m % 2, :]

    def rank_row(dev_row, dev_col):
        before = (dev_row == dev_col) & (iota((ENDS, ENDS), 0) < iota((ENDS, ENDS), 1))
        return jnp.sum(jnp.where(before, 1.0, 0.0), axis=0, keepdims=True).astype(jnp.int32)

    def rank_col(dev_row, dev_col, pos_row, pos_col):
        before = (dev_row == dev_col) & (pos_row < pos_col)
        return jnp.sum(jnp.where(before, 1.0, 0.0), axis=1, keepdims=True).astype(jnp.int32)

    peer_row, peer_col = turned[32, 0:1], mine[:, 256:257]
    line_row, line_col = turned[32, 2:3], mine[:, 258:259]
    peer_rank = rank_row(peer_row, peer_col)
    line_rank = rank_row(line_row, line_col)
    peer_rank_in = rank_col(peer_row, peer_col, turned[32, 1:2], mine[:, 257:258])
    line_rank_in = rank_col(end_owner[0:1], end_dev_col, end_owner[1:2], end_pos_col)
    to_peer[...] = hot(iota((DEVICES, ENDS), 0) == peer_row.astype(jnp.int32))
    to_line[...] = hot(iota((DEVICES, ENDS), 0) == line_row.astype(jnp.int32))
    from_peer[...] = hot(iota((ENDS, DEVICES), 1) == peer_col.astype(jnp.int32))
    from_line[...] = hot(iota((ENDS, DEVICES), 1) == end_dev_col.astype(jnp.int32))
    worst_rank = jnp.maximum(
        jnp.max(peer_rank, axis=1, keepdims=True), jnp.max(line_rank, axis=1, keepdims=True)
    )
    over = jnp.where(worst_rank >= SLOTS, 1.0, 0.0)
    flag_lane = jnp.where(lane == 127, 1.0, 0.0) * over
    mode_pick = hot(lax.rem(iota((8, 256), 1), 128) // SLOTS == iota((8, 256), 0))

    for src_z in range(3):
        @pl.when(z != src_z)
        def _wait():
            drain(block.at[src_z], block_sems.at[src_z])
            drain(v0.at[src_z], v0_sems.at[src_z])

        @pl.when(z == src_z)
        def _own():
            drain(block.at[src_z], own_sem.at[0])

    def build(sub, carry):
        for src_z in range(3):
            high, low = split(block[src_z, sub])
            solve[sub, src_z * 128:(src_z + 1) * 128] = high
            solve[sub, 384 + src_z * 128:512 + src_z * 128] = low
        return carry

    lax.fori_loop(0, 4, build, 0)

    def to_rows(values, rank, onehot):
        spread = jnp.concatenate(
            [jnp.broadcast_to(values[j:j + 1], (SLOTS, ENDS)) for j in range(6)]
            + [jnp.zeros((2 * SLOTS, ENDS), F32)], axis=0
        )
        slot = lax.rem(iota((DEVICES, ENDS), 0), SLOTS)
        high, low = split(jnp.where(slot == rank, spread, 0.0))
        rows = dot_nt(onehot[...], jnp.concatenate([high, low], axis=0))
        return rows[:, :128] + rows[:, 128:]

    def from_rows(rows, rank, onehot):
        high, low = split(rows)
        found = jnp.dot(onehot[...], jnp.concatenate([high, low], axis=1), preferred_element_type=F32)
        slot = lax.rem(iota((ENDS, 256), 1), SLOTS)
        found = jnp.where(slot == rank, found, 0.0).astype(BF16)
        return dot_nt(mode_pick, found)

    def take_currents(n):
        drain(cur_recv.at[n, pl.ds(0, DEVICES - 1)], cur_sems.at[n])
        found = from_rows(cur_recv[n].reshape(DEVICES, 128), line_rank_in, from_line)
        lines_out[n, 0] = found[0:6, 0:128]
        lines_out[n, 1] = found[0:6, 128:256]

    def step(n, carry):
        delayed, worst = carry
        hist = hacc[n] + ht[1] * delayed
        phase = [jnp.sum(mmap[k] * hist, axis=0, keepdims=True) for k in range(6)]
        pieces = jnp.concatenate(
            [p[:, t * 128:(t + 1) * 128] for t in range(2) for p in phase], axis=0
        )
        turned = pltpu.roll(pieces, 64, 1)
        inj[z, n, 0:12] = pieces
        tiles = []
        for t in range(2):
            for h in range(2):
                even, odd = (turned, pieces) if h else (pieces, turned)
                rows = [
                    jnp.where(lane < 64, even[t * 6 + 2 * u:t * 6 + 2 * u + 1], odd[t * 6 + 2 * u + 1:t * 6 + 2 * u + 2])
                    for u in range(3)
                ]
                high, low = split(jnp.concatenate(rows, axis=1))
                both = dot_nt(jnp.concatenate([high, low], axis=0), solve[2 * t + h])
                both = both[0:1] + both[1:2]
                tiles += [
                    both[:, u * 128:(u + 1) * 128] + both[:, 384 + u * 128:512 + u * 128]
                    + v0[u, 2 * t + h, pl.ds(n, 1), :]
                    for u in range(3)
                ]
        volts = jnp.concatenate(tiles, axis=0)
        swung = pltpu.roll(volts, 64, 1)
        modal = jnp.zeros((8, ENDS), F32)
        for k in range(6):
            left, right = (swung, volts) if k % 2 else (volts, swung)
            row = jnp.concatenate(
                [
                    jnp.where(
                        lane < 64, left[6 * t + k // 2:6 * t + k // 2 + 1], right[6 * t + 3 + k // 2:6 * t + 4 + k // 2]
                    )
                    for t in range(2)
                ], axis=1
            )
            modal = modal + mmap[k] * row
        charac = cacc[n] + g[0] * modal
        wave = 2.0 * charac - hist

        @pl.when(n < STEPS - 1)
        def _waves():
            wave_send[n] = (to_rows(wave, peer_rank, to_peer) + flag_lane)[:, None, :]
            send_all(lambda d: wave_send.at[n, d], wave_recv.at[n, me], wave_sems.at[0, n], wave_sems.at[1, n])
            wave_recv[n, me] = wave_send[n, me]

        cur_send[n] = to_rows(charac - hist, line_rank, to_line)[:, None, :]
        send_all(lambda d: cur_send.at[n, d], cur_recv.at[n, me], cur_sems.at[STEPS + n], cur_sems.at[n])
        cur_recv[n, me] = cur_send[n, me]

        @pl.when(lax.rem(n, 4) == 3)
        def _injections():
            part = inj.at[z, pl.ds(n - 3, 4)]
            for k in range(1, 8):
                nz = lax.rem(z + k, 8)
                pltpu.make_async_remote_copy(
                    src_ref=part, dst_ref=part, send_sem=inj_sems.at[0], recv_sem=inj_sems.at[1],
                    device_id=(i, nz), device_id_type=MESH,
                ).start()

        for k in range(2, STEPS):
            hacc[n + k - 1] = hacc[n + k - 1] + ht[k] * delayed
        for k in range(1, STEPS):
            cacc[n + k] = cacc[n + k] + g[k] * modal

        @pl.when(n > 0)
        def _lines():
            take_currents(n - 1)

        last = jnp.minimum(n, STEPS - 2)

        @pl.when(n < STEPS - 1)
        def _arrive():
            drain(wave_recv.at[n, pl.ds(0, DEVICES - 1)], wave_sems.at[1, n])

        rows = wave_recv[last].reshape(DEVICES, 128)
        worst = jnp.maximum(worst, jnp.max(rows[:, 127:128], axis=0, keepdims=True))
        return from_rows(rows, peer_rank_in, from_peer), worst

    delayed, worst = lax.fori_loop(0, STEPS, step, (jnp.zeros((8, ENDS), F32), jnp.zeros((1, 1), F32)))
    flag_out[...] = worst

    drain(inj.at[pl.ds(0, 7)], inj_sems.at[1])

    def finish(a, carry):
        for t in range(2):
            tiles = [inj[a, :, t * 6 + k, :] for k in range(6)]
            for h in range(2):
                s = a * 4 + t * 2 + h
                left = []
                for u in range(3):
                    even, odd = tiles[2 * u], tiles[2 * u + 1]
                    if h == 0:
                        left.append(jnp.where(lane < 64, even, pltpu.roll(odd, 64, 1)))
                    else:
                        left.append(jnp.where(lane < 64, pltpu.roll(even, 64, 1), odd))
                high, low = split(jnp.concatenate(left, axis=1))
                both = dot_nt(jnp.concatenate([high, low], axis=0), fixed[s])
                both = both[:STEPS] + both[STEPS:]
                total = still[s] + both[:, :128] + both[:, 128:]
                live = lane + z * 128 < counts[s]
                volts_out[:, pl.ds(s, 1), :] = jnp.where(live, total, 0.0)[:, None, :]
        return carry

    lax.fori_loop(0, 8, finish, 0)
    take_currents(STEPS - 1)

    drain(code_send.at[pl.ds(0, DEVICES - 1)], code_sems.at[0])
    drain(table_send.at[pl.ds(0, DEVICES - 1)], table_sems.at[0])
    drain(port_send.at[pl.ds(0, 7)], port_sems.at[0])
    drain(inj.at[pl.ds(0, 7)], inj_sems.at[0])

    def sent(n, carry):
        drain(cur_send.at[n, pl.ds(0, DEVICES - 1)], cur_sems.at[STEPS + n])

        @pl.when(n < STEPS - 1)
        def _wave():
            drain(wave_send.at[n, pl.ds(0, DEVICES - 1)], wave_sems.at[0, n])
        return carry

    lax.fori_loop(0, STEPS, sent, 0)

    @pl.when(z >= 4)
    def _relayed():
        drain(relay, relay_sems.at[2])

    @pl.when(z < 3)
    def _sent():
        drain(still.at[pl.ds(0, 28)], v0_sems.at[3])
        drain(inverses.at[pl.ds(0, 28), :, pl.ds(0, 384)], block_sems.at[3])


def run_steps(*operands):
    vm = pl.BlockSpec(memory_space=pltpu.VMEM)
    dma = pltpu.SemaphoreType.DMA
    rows = (STEPS, DEVICES, 1, 128)
    return pl.pallas_call(
        steps_kernel,
        out_shape=(
            jax.ShapeDtypeStruct((STEPS, 32, 128), F32),
            jax.ShapeDtypeStruct((STEPS, 2, 6, 128), F32),
            jax.ShapeDtypeStruct((1, 1), F32),
        ),
        in_specs=[pl.BlockSpec(memory_space=pl.ANY), pl.BlockSpec(memory_space=pltpu.SMEM)] + [vm] * (len(operands) - 2),
        out_specs=(vm, vm, vm),
        scratch_shapes=[
            pltpu.VMEM((2, 6, 30, 128), F32),
            pltpu.VMEM((2, 6, 30, 128), F32),
            pltpu.VMEM((6, 30, 128), F32),
            pltpu.VMEM((6, 30, 128), F32),
            pltpu.VMEM((STEPS, 6, 128), F32),
            pltpu.VMEM((64, 8, ENDS), F32),
            pltpu.VMEM((DEVICES, 1, 128), F32),
            pltpu.VMEM((DEVICES, 1, 128), F32),
            pltpu.VMEM((DEVICES, 8, 512), F32),
            pltpu.VMEM((DEVICES, 8, 512), F32),
            pltpu.VMEM((8, 4, 8, 512), F32),
            pltpu.VMEM((4, 8, 8, 512), F32),
            pltpu.VMEM((2, 4, 128, 1024), F32),
            pltpu.VMEM((32, 256, 384), BF16),
            pltpu.VMEM((32, STEPS, 128), F32),
            pltpu.VMEM((3, 4, STEPS, 128), F32),
            pltpu.VMEM((3, 4, 128, 384), F32),
            pltpu.VMEM((4, 128, 384), F32),
            pltpu.VMEM((4, 768, 384), BF16),
            pltpu.VMEM((6, 8, ENDS), F32),
            pltpu.VMEM((32, 8, ENDS), F32),
            pltpu.VMEM((32, 8, ENDS), F32),
            pltpu.VMEM((STEPS, 8, ENDS), F32),
            pltpu.VMEM((STEPS, 8, ENDS), F32),
            pltpu.VMEM((DEVICES, ENDS), BF16),
            pltpu.VMEM((ENDS, DEVICES), BF16),
            pltpu.VMEM((DEVICES, ENDS), BF16),
            pltpu.VMEM((ENDS, DEVICES), BF16),
            pltpu.VMEM(rows, F32),
            pltpu.VMEM(rows, F32),
            pltpu.VMEM(rows, F32),
            pltpu.VMEM(rows, F32),
            pltpu.VMEM((8, STEPS, 16, 128), F32),
            dma((2,)), dma((2,)), dma((2,)), dma((2,)), dma((4,)), dma((4,)), dma((3,)), dma((1,)), dma((2, STEPS)),
            dma((2 * STEPS,)), dma((2,)),
        ],
        compiler_params=pltpu.CompilerParams(collective_id=0, has_side_effects=True, vmem_limit_bytes=VMEM_CAP),
        name="transient_steps",
    )(*operands)


def body(
    inverses, node_counts, sources, port_slot, end_slot, modal_map, delay_steps, wave_buffer, yc_decay, yc_residue,
    yc_direct, yc_state, prop_decay, prop_residue, prop_state,
):
    volts, lines, flag = run_steps(
        inverses, node_counts, sources, port_slot.reshape(1, -1), end_slot.reshape(1, -1), modal_map, delay_steps,
        wave_buffer, yc_decay, yc_residue, yc_direct, yc_state.transpose(1, 2, 0, 3), prop_decay, prop_residue,
        prop_state.transpose(1, 2, 0, 3),
    )

    def quick(_):
        return volts, lines

    def general(_):
        return general_body(
            inverses, node_counts, sources, port_slot, end_slot, modal_map, delay_steps, wave_buffer, yc_decay,
            yc_residue, yc_direct, yc_state, prop_decay, prop_residue, prop_state,
        )

    return lax.cond(flag[0, 0] > 0.0, general, quick, 0)


def read_delayed(extended, delay_steps, step_index, buffer_len):
    read_at = buffer_len + step_index - delay_steps
    depth = jnp.arange(extended.shape[2], dtype=jnp.int32)
    picker = (depth[None, :, None] == read_at[:, None, :]).astype(extended.dtype)
    return jnp.sum(extended * picker[None], axis=2)


def move_back(outgoing):
    returned = lax.all_to_all(outgoing, ("net", "line"), split_axis=1, concat_axis=1, tiled=True)
    return returned


def move_forward(sending):
    arrived = lax.all_to_all(sending, ("net", "line"), split_axis=1, concat_axis=1, tiled=True)
    return arrived


def general_body(
    inverses,
    node_counts,
    sources,
    port_slot,
    end_slot,
    modal_map,
    delay_steps,
    wave_buffer,
    yc_decay,
    yc_residue,
    yc_direct,
    yc_state,
    prop_decay,
    prop_residue,
    prop_state,
):
    net_size = lax.axis_size("net")
    line_size = lax.axis_size("line")
    device_count = net_size * line_size
    sub_count, row_count, node_total = inverses.shape
    step_count = sources.shape[0]
    port_cols = port_slot.shape[1]
    mode_count = modal_map.shape[0]
    line_count = end_slot.shape[1]
    buffer_len = wave_buffer.shape[2]
    port_total = port_cols * line_size
    slot_cap = max(2, 4 * sub_count * port_cols // device_count)
    slot_width = device_count * slot_cap
    line_pos = lax.axis_index("line")
    row_ids = line_pos * row_count + jnp.arange(row_count, dtype=jnp.int32)
    live_mask = row_ids[None, :] < node_counts[:, None]
    port_flat = port_slot.reshape(-1)
    end_flat = end_slot.reshape(-1)
    used_nodes = port_total * mode_count
    first_port = line_pos * port_cols
    extended = jnp.concatenate(
        [wave_buffer, jnp.zeros((2, mode_count, step_count, line_count), jnp.float32)], axis=2
    )
    volts_init = jnp.zeros((step_count, sub_count, row_count), jnp.float32)
    currents_init = jnp.zeros((step_count, 2, mode_count, line_count), jnp.float32)

    def advance(step_index, carried):
        yc_now, prop_now, extended, volts_acc, currents_acc = carried
        delayed = read_delayed(extended, delay_steps, step_index, buffer_len)
        prop_now = prop_decay[None] * prop_now + prop_residue[None] * delayed[::-1][:, :, None, :]
        history = jnp.sum(prop_now, axis=2)
        history_phase = jnp.sum(modal_map[None] * history[:, None], axis=2)
        outgoing = (
            jnp.zeros((mode_count, slot_width), jnp.float32)
            .at[:, end_flat]
            .set(history_phase.transpose(1, 0, 2).reshape(mode_count, 2 * line_count))
        )
        returned = move_back(outgoing)
        own_ports = (
            returned[:, port_flat]
            .reshape(mode_count, sub_count, port_cols)
            .transpose(1, 2, 0)
            .reshape(sub_count, port_cols * mode_count)
        )
        port_currents = lax.all_gather(own_ports, "line", axis=1, tiled=True)
        port_currents = (
            port_currents.reshape(sub_count, port_total, mode_count)
            .transpose(0, 2, 1)
            .reshape(sub_count, used_nodes)
        )
        source_now = lax.dynamic_index_in_dim(sources, step_index, 0, keepdims=False)
        injection = source_now + jnp.pad(port_currents, ((0, 0), (0, node_total - used_nodes)))
        solved = jnp.einsum("src,sc->sr", inverses, injection, precision=lax.Precision.HIGHEST)
        solved = jnp.where(live_mask, solved, 0.0)
        gathered = lax.all_gather(solved, "line", axis=1, tiled=True)
        by_mode = gathered[:, :used_nodes].reshape(sub_count, mode_count, port_total)
        own_volts = lax.dynamic_slice_in_dim(by_mode, first_port, port_cols, 2)
        own_volts = own_volts.transpose(1, 0, 2).reshape(mode_count, sub_count * port_cols)
        sending = jnp.zeros((mode_count, slot_width), jnp.float32).at[:, port_flat].set(own_volts)
        arrived = move_forward(sending)
        end_volts = arrived[:, end_flat].reshape(mode_count, 2, line_count)
        modal_volts = jnp.sum(modal_map[:, :, None, :] * end_volts[:, None], axis=0).transpose(
            1, 0, 2
        )
        yc_now = yc_decay[None] * yc_now + yc_residue[None] * modal_volts[:, :, None, :]
        charac = yc_direct[None] * modal_volts + jnp.sum(yc_now, axis=2)
        current = charac - history
        wave_out = 2.0 * charac - history
        extended = lax.dynamic_update_slice_in_dim(
            extended, wave_out[:, :, None, :], buffer_len + step_index, 2
        )
        volts_acc = lax.dynamic_update_slice_in_dim(volts_acc, solved[None], step_index, 0)
        currents_acc = lax.dynamic_update_slice_in_dim(currents_acc, current[None], step_index, 0)
        return (yc_now, prop_now, extended, volts_acc, currents_acc)

    final = lax.fori_loop(
        0, step_count, advance, (yc_state, prop_state, extended, volts_init, currents_init)
    )
    return (final[3], final[4])


def solution(mesh):
    placed = (
        P("net", "line", None),
        P("net"),
        P(None, "net", None),
        P("net", "line"),
        P(None, ("net", "line")),
        P(None, None, ("net", "line")),
        P(None, ("net", "line")),
        P(None, None, None, ("net", "line")),
        P(None, None, ("net", "line")),
        P(None, None, ("net", "line")),
        P(None, ("net", "line")),
        P(None, None, None, ("net", "line")),
        P(None, None, ("net", "line")),
        P(None, None, ("net", "line")),
        P(None, None, None, ("net", "line")),
    )
    return jax.shard_map(
        body,
        mesh=mesh,
        in_specs=placed,
        out_specs=(P(None, "net", "line"), P(None, None, None, ("net", "line"))),
        check_vma=False,
    )
```

```python
import jax
import jax.numpy as jnp
from jax import lax
from jax.experimental import pallas as pl
from jax.experimental.pallas import tpu as pltpu
from jax.sharding import PartitionSpec as P

MESH = pl.DeviceIdType.MESH
VMEM_CAP = 58 * 1024 * 1024
DEVICES = 128
SLOTS = 16
PACK = 64
ENDS = 256
STEPS = 16
F32 = jnp.float32
BF16 = jnp.bfloat16
RING = (0, 1, 2, 1)
OFFSETS = sorted(
    [(a, b, c, e) for a in range(4) for b in range(4) for c in range(4) for e in range(2) if (a, b, c, e) != (0, 0, 0, 0)],
    key=lambda o: -(RING[o[0]] + RING[o[1]] + RING[o[2]] + 2 * o[3]),
)


def peer(i, z, offset):
    dy, dx, dz, dc = offset
    y, x, zz, c = i // 4, lax.rem(i, 4), z // 2, lax.rem(z, 2)
    ni = lax.rem(y + dy, 4) * 4 + lax.rem(x + dx, 4)
    nz = lax.rem(zz + dz, 4) * 2 + lax.rem(c + dc, 2)
    return ni, nz


def drain(ref, sem):
    pltpu.make_async_copy(ref, ref, sem).wait()


def split(value):
    high = value.astype(BF16)
    low = (value - high.astype(F32)).astype(BF16)
    return high, low


def dot_nt(left, right):
    return lax.dot_general(left, right, (((1,), (1,)), ((), ())), preferred_element_type=F32)


def iota(shape, dim):
    return lax.broadcasted_iota(jnp.int32, shape, dim)


def hot(condition):
    return jnp.where(condition, 1.0, 0.0).astype(BF16)


def steps_kernel(
    inverses, counts, sources, port_row, end_row, mmap_in, delay, waves, yd, yr, ydir, ys_in, pd, pr, ps_in,
    volts_out, lines_out, flag_out,
    yst, pst, yim, pim, hbuf, table, code_send, code_recv, table_send, table_recv, port_send, own_recv,
    chunk, fixed, still, v0, block, relay, solve, mmap, hacc, cacc, ht, g,
    to_peer, from_peer, to_line, from_line, wave_send, wave_recv, cur_send, cur_recv, inj,
    code_sems, table_sems, port_sems, chunk_sem, v0_sems, block_sems, relay_sems, own_sem, wave_sems, cur_sems, inj_sems,
):
    i = lax.axis_index("net")
    z = lax.axis_index("line")
    me = i * 8 + z
    lane = iota((1, 128), 1)
    barrier = pltpu.get_barrier_semaphore()
    for offset in OFFSETS:
        pl.semaphore_signal(barrier, inc=1, device_id=peer(i, z, offset), device_id_type=MESH)

    def send_all(src_of, dst, sends, recvs):
        for offset in OFFSETS:
            ni, nz = peer(i, z, offset)
            pltpu.make_async_remote_copy(
                src_ref=src_of(ni * 8 + nz), dst_ref=dst, send_sem=sends, recv_sem=recvs,
                device_id=(ni, nz), device_id_type=MESH,
            ).start()

    def chunk_copy(c, slot):
        return pltpu.make_async_copy(inverses.at[pl.ds(c * 4, 4)], chunk.at[slot], chunk_sem.at[slot])

    chunk_copy(0, 0).start()

    def column(row):
        return jnp.broadcast_to(row.astype(F32), (128, ENDS)).T[:, 0:1].astype(jnp.int32)

    end_col = column(end_row[...])

    f = iota((1, ENDS), 1)
    owner_dev = (i * 8 + f // 32).astype(F32)
    owner_pos = (lax.rem(f // 8, 4) * 64 + z * 8 + lax.rem(f, 8)).astype(F32)
    code_row = iota((128, ENDS), 0)
    codes = jnp.where(
        lax.rem(code_row, 8) == lax.rem(port_row[...], 8),
        jnp.where(code_row < 8, owner_dev, jnp.where(code_row < 16, owner_pos, 0.0)), 0.0,
    ).astype(BF16)
    code_send[...] = dot_nt(hot(iota((DEVICES, ENDS), 0) == port_row[...] // 8), codes)[:, None, :]

    pl.semaphore_wait(barrier, len(OFFSETS))
    send_all(lambda d: code_send.at[d], code_recv.at[me], code_sems.at[0], code_sems.at[1])
    code_recv[me] = code_send[me]

    chip, core = z // 2, lax.rem(z, 2)

    def block_piece(dz, dc, first, count):
        nz = lax.rem(chip + dz, 4) * 2 + lax.rem(core + dc, 2)
        pltpu.make_async_remote_copy(
            src_ref=inverses.at[pl.ds(nz * 4 + first, count), :, pl.ds(0, 384)],
            dst_ref=block.at[z, pl.ds(first, count)], send_sem=block_sems.at[3], recv_sem=block_sems.at[z],
            device_id=(i, nz), device_id_type=MESH,
        ).start()

    @pl.when(z < 2)
    def _two_hops():
        for dc in range(2):
            nz = 4 + lax.rem(core + dc, 2)
            pltpu.make_async_remote_copy(
                src_ref=inverses.at[pl.ds(nz * 4 + 2, 2), :, pl.ds(0, 384)], dst_ref=relay.at[pl.ds(z * 2, 2)],
                send_sem=block_sems.at[3], recv_sem=relay_sems.at[z],
                device_id=(i, nz + 2), device_id_type=MESH,
            ).start()
            block_piece(2, dc, 0, 2)

    @pl.when(z == 2)
    def _two_hops_whole():
        for dc in range(2):
            nz = 6 + dc
            pltpu.make_async_remote_copy(
                src_ref=inverses.at[pl.ds(nz * 4, 4), :, pl.ds(0, 384)], dst_ref=relay,
                send_sem=block_sems.at[3], recv_sem=relay_sems.at[0],
                device_id=(i, nz - 2), device_id_type=MESH,
            ).start()

    @pl.when(z < 3)
    def _own():
        pltpu.make_async_copy(inverses.at[pl.ds(z * 4, 4), :, pl.ds(0, 384)], block.at[z], own_sem.at[0]).start()

    table[...] = jnp.zeros(table.shape, F32)
    for e in range(2):
        yst[e] = ys_in[:, :, e, :]
        pst[e] = ps_in[:, :, e, :]
    yim[...] = yr[...]
    pim[...] = pr[...]
    depth = iota((6, 64, 128), 1)

    def respond(n, carry):
        pick = depth == (64 + n - delay[...])[:, None, :]
        ydec, pdec, pres = yd[...], pd[...], pr[...]
        for e in range(2):
            seen = jnp.sum(jnp.where(pick, waves[1 - e], 0.0), axis=1)
            now = pdec * pst[e] + pres * seen[:, None, :]
            pst[e] = now
            table[n, 0:6, e * 128:(e + 1) * 128] = jnp.sum(now, axis=1)
            free = ydec * yst[e]
            yst[e] = free
            table[16 + n, 0:6, e * 128:(e + 1) * 128] = jnp.sum(free, axis=1)
        first = jnp.where(n == 0, 1.0, 0.0)
        pnow, ynow = pim[...], yim[...]
        hbuf[n] = jnp.sum(pnow, axis=1)
        gnow = jnp.sum(ynow, axis=1) + first * ydir[...]
        table[48 + n, 0:6, 0:128] = gnow
        table[48 + n, 0:6, 128:256] = gnow
        pim[...] = pnow * pdec
        yim[...] = ynow * ydec
        return carry

    lax.fori_loop(0, STEPS, respond, 0)
    lag = delay[...]
    for k in range(1, STEPS):
        total = jnp.zeros((6, 128), F32)
        for m in range(k):
            total = total + jnp.where(lag == k - m, hbuf[m], 0.0)
        table[32 + k, 0:6, 0:128] = total
        table[32 + k, 0:6, 128:256] = total
    for k in range(6):
        for j in range(6):
            m = k * 6 + j
            row = mmap_in[k, j:j + 1, :]
            table[m // 2, 6 + m % 2:7 + m % 2, 0:128] = row
            table[m // 2, 6 + m % 2:7 + m % 2, 128:256] = row

    drain(code_recv.at[pl.ds(0, DEVICES - 1)], code_sems.at[1])
    got = code_recv[...].reshape(DEVICES, 128).astype(BF16)
    found = jnp.dot(hot(iota((ENDS, DEVICES), 1) == end_col // 8), got, preferred_element_type=F32)
    code_lane = iota((ENDS, 128), 1)
    found = jnp.where(
        (lax.rem(code_lane, 8) == lax.rem(end_col, 8)) & (code_lane < 16), found, 0.0
    ).astype(BF16)
    end_owner = dot_nt(hot(iota((8, 128), 1) // 8 == iota((8, 128), 0)), found)
    found_col = found.astype(F32)
    end_dev_col = jnp.sum(jnp.where(code_lane < 8, found_col, 0.0), axis=1, keepdims=True)
    end_pos_col = jnp.sum(jnp.where(code_lane >= 8, found_col, 0.0), axis=1, keepdims=True)
    partner = jnp.concatenate([end_owner[0:2, 128:], end_owner[0:2, :128]], axis=1)
    table[32, 0:2, :] = partner
    table[32, 2:3, :] = jnp.full((1, ENDS), me).astype(F32)
    table[32, 3:4, :] = f.astype(F32)
    table[32, 4:6, :] = end_owner[0:2]
    table[32, 6:7, :] = jnp.ones((1, ENDS), F32)

    high, low = split(table[...].reshape(512, ENDS))
    parts = jnp.concatenate([high, low], axis=0)

    def fill(c, carry):
        pick = hot(iota((256, ENDS), 0) + c * 256 == end_row[...])
        rows = dot_nt(pick, parts)
        table_send[pl.ds(c * 32, 32)] = (rows[:, :512] + rows[:, 512:]).reshape(32, 8, 512)
        return carry

    lax.fori_loop(0, 4, fill, 0)
    for dy, dx in sorted([(a, b) for a in range(4) for b in range(4)], key=lambda o: -(RING[o[0]] + RING[o[1]]))[:15]:
        ni, _ = peer(i, z, (dy, dx, 0, 0))
        pltpu.make_async_remote_copy(
            src_ref=table_send.at[pl.ds(ni * 8, 8)], dst_ref=table_recv.at[pl.ds(i * 8, 8)],
            send_sem=table_sems.at[0], recv_sem=table_sems.at[1], device_id=(ni, z), device_id_type=MESH,
        ).start()
    table_recv[pl.ds(i * 8, 8)] = table_send[pl.ds(i * 8, 8)]

    @pl.when(z < 3)
    def _second_part():
        block_piece(0, 1, 0, 4)
        block_piece(1, 0, 0, 4)
        block_piece(3, 0, 0, 4)

    def solve_sources(c, carry):
        slot = lax.rem(c, 2)
        chunk_copy(c, slot).wait()

        @pl.when(c < 7)
        def _next():
            chunk_copy(c + 1, 1 - slot).start()

        def one(s, carry):
            a_high, a_low = split(chunk[slot, s])
            matrix = jnp.concatenate([a_high, a_low], axis=0)
            fixed[c * 4 + s] = matrix[:, :384]
            s_high, s_low = split(sources[:, pl.ds(c * 4 + s, 1), :].reshape(STEPS, 1024))
            both = dot_nt(jnp.concatenate([s_high, s_low], axis=0), matrix)
            both = both[:STEPS] + both[STEPS:]
            still[c * 4 + s] = both[:, :128] + both[:, 128:]
            return carry

        lax.fori_loop(0, 4, one, 0)
        @pl.when((z < 3) & (c != z))
        def _send():
            pltpu.make_async_remote_copy(
                src_ref=still.at[pl.ds(c * 4, 4)], dst_ref=v0.at[z], send_sem=v0_sems.at[3], recv_sem=v0_sems.at[z],
                device_id=(i, c), device_id_type=MESH,
            ).start()

        @pl.when((z < 3) & (c == z))
        def _keep():
            v0[z] = still[pl.ds(c * 4, 4)]

        return carry

    lax.fori_loop(0, 8, solve_sources, 0)

    @pl.when(z >= 6)
    def _relay():
        for src_z in range(2):
            part = relay.at[pl.ds(src_z * 2, 2)]
            drain(part, relay_sems.at[src_z])
            pltpu.make_async_remote_copy(
                src_ref=part, dst_ref=block.at[src_z, pl.ds(2, 2)], send_sem=relay_sems.at[2],
                recv_sem=block_sems.at[src_z], device_id=(i, z - 2), device_id_type=MESH,
            ).start()

    @pl.when((z == 4) | (z == 5))
    def _relay_up():
        drain(relay, relay_sems.at[0])
        pltpu.make_async_remote_copy(
            src_ref=relay, dst_ref=block.at[2], send_sem=relay_sems.at[2], recv_sem=block_sems.at[2],
            device_id=(i, z + 2), device_id_type=MESH,
        ).start()

    meta_pick = hot(iota((8, 512), 1) == 256 + iota((8, 512), 0))
    drain(table_recv.at[pl.ds(0, DEVICES - 8)], table_sems.at[1])
    meta = jnp.concatenate(
        [dot_nt(meta_pick, table_recv[c * 32:(c + 1) * 32].reshape(256, 512).astype(BF16)) for c in range(4)], axis=1
    )
    target = (meta[4:5].astype(jnp.int32) - i * 8)
    held = meta[6:7] > 0.5
    chosen = (iota((8, 1024), 0) == target) & held
    chosen_hot = hot(chosen)
    ahead = jnp.concatenate(
        [
            jnp.dot(chosen_hot, hot(iota((1024, 256), 0) < iota((1024, 256), 1) + c * 256), preferred_element_type=F32)
            for c in range(4)
        ], axis=1
    )
    place = jnp.sum(jnp.where(chosen, ahead, 0.0), axis=0, keepdims=True).astype(jnp.int32)
    pack_over = jnp.max(place, axis=1, keepdims=True) >= PACK
    key = jnp.where(held & (place < PACK), target * PACK + place, -1)
    packed = jnp.zeros((8 * PACK, 1024), F32)
    for c in range(4):
        high, low = split(table_recv[c * 32:(c + 1) * 32].reshape(256, 512))
        pick = hot(iota((8 * PACK, 256), 0) == key[:, c * 256:(c + 1) * 256])
        packed = packed + jnp.dot(pick, jnp.concatenate([high, low], axis=1), preferred_element_type=F32)
    port_send[...] = (packed[:, :512] + packed[:, 512:]).reshape(8, PACK, 512)
    for k in range(1, 8):
        nz = lax.rem(z + k, 8)
        pltpu.make_async_remote_copy(
            src_ref=port_send.at[nz], dst_ref=own_recv.at[z], send_sem=port_sems.at[0], recv_sem=port_sems.at[1],
            device_id=(i, nz), device_id_type=MESH,
        ).start()
    own_recv[z] = port_send[z]

    @pl.when(z < 3)
    def _third_part():
        for first in (0, 2):
            block_piece(1, 1, first, 2)
            block_piece(3, 1, first, 2)

    drain(own_recv.at[pl.ds(0, 7)], port_sems.at[1])

    high, low = split(own_recv[...].reshape(8 * PACK, 512))
    meta = dot_nt(meta_pick, high)
    spot = jnp.where(meta[6:7] > 0.5, meta[5:6].astype(jnp.int32), -1)
    pick = hot(iota((ENDS, 8 * PACK), 0) == spot)
    mine = jnp.dot(pick, jnp.concatenate([high, low], axis=1), preferred_element_type=F32)
    mine = mine[:, :512] + mine[:, 512:]
    turned = mine.T.reshape(64, 8, ENDS)
    real = iota((1, 8, ENDS), 1) < 6
    hacc[...] = jnp.zeros(hacc.shape, F32)
    cacc[...] = jnp.zeros(cacc.shape, F32)
    hacc[0:STEPS] = jnp.where(real, turned[0:16], 0.0)
    cacc[0:STEPS] = jnp.where(real, turned[16:32], 0.0)
    ht[...] = jnp.where(real, turned[32:48], 0.0)
    g[...] = jnp.where(real, turned[48:64], 0.0)
    mmap[...] = jnp.zeros(mmap.shape, F32)
    for k in range(6):
        for j in range(6):
            m = k * 6 + j
            mmap[k, j:j + 1, :] = turned[m // 2, 6 + m % 2:7 + m % 2, :]

    def rank_row(dev_row, dev_col):
        before = (dev_row == dev_col) & (iota((ENDS, ENDS), 0) < iota((ENDS, ENDS), 1))
        return jnp.sum(jnp.where(before, 1.0, 0.0), axis=0, keepdims=True).astype(jnp.int32)

    def rank_col(dev_row, dev_col, pos_row, pos_col):
        before = (dev_row == dev_col) & (pos_row < pos_col)
        return jnp.sum(jnp.where(before, 1.0, 0.0), axis=1, keepdims=True).astype(jnp.int32)

    peer_row, peer_col = turned[32, 0:1], mine[:, 256:257]
    line_row, line_col = turned[32, 2:3], mine[:, 258:259]
    peer_rank = rank_row(peer_row, peer_col)
    line_rank = rank_row(line_row, line_col)
    peer_rank_in = rank_col(peer_row, peer_col, turned[32, 1:2], mine[:, 257:258])
    line_rank_in = rank_col(end_owner[0:1], end_dev_col, end_owner[1:2], end_pos_col)
    to_peer[...] = hot(iota((DEVICES, ENDS), 0) == peer_row.astype(jnp.int32))
    to_line[...] = hot(iota((DEVICES, ENDS), 0) == line_row.astype(jnp.int32))
    from_peer[...] = hot(iota((ENDS, DEVICES), 1) == peer_col.astype(jnp.int32))
    from_line[...] = hot(iota((ENDS, DEVICES), 1) == end_dev_col.astype(jnp.int32))
    worst_rank = jnp.maximum(
        jnp.max(peer_rank, axis=1, keepdims=True), jnp.max(line_rank, axis=1, keepdims=True)
    )
    over = jnp.where((worst_rank >= SLOTS) | pack_over, 1.0, 0.0)
    flag_lane = jnp.where(lane == 127, 1.0, 0.0) * over
    mode_pick = hot(lax.rem(iota((8, 256), 1), 128) // SLOTS == iota((8, 256), 0))

    for src_z in range(3):
        @pl.when(z != src_z)
        def _wait():
            drain(block.at[src_z], block_sems.at[src_z])
            drain(v0.at[src_z], v0_sems.at[src_z])

        @pl.when(z == src_z)
        def _own():
            drain(block.at[src_z], own_sem.at[0])

    def build(sub, carry):
        for src_z in range(3):
            high, low = split(block[src_z, sub])
            solve[sub, src_z * 128:(src_z + 1) * 128] = high
            solve[sub, 384 + src_z * 128:512 + src_z * 128] = low
        return carry

    lax.fori_loop(0, 4, build, 0)

    def to_rows(values, rank, onehot):
        spread = jnp.concatenate(
            [jnp.broadcast_to(values[j:j + 1], (SLOTS, ENDS)) for j in range(6)]
            + [jnp.zeros((2 * SLOTS, ENDS), F32)], axis=0
        )
        slot = lax.rem(iota((DEVICES, ENDS), 0), SLOTS)
        high, low = split(jnp.where(slot == rank, spread, 0.0))
        rows = dot_nt(onehot[...], jnp.concatenate([high, low], axis=0))
        return rows[:, :128] + rows[:, 128:]

    def from_rows(rows, rank, onehot):
        high, low = split(rows)
        found = jnp.dot(onehot[...], jnp.concatenate([high, low], axis=1), preferred_element_type=F32)
        slot = lax.rem(iota((ENDS, 256), 1), SLOTS)
        found = jnp.where(slot == rank, found, 0.0).astype(BF16)
        return dot_nt(mode_pick, found)

    def take_currents(n):
        drain(cur_recv.at[n, pl.ds(0, DEVICES - 1)], cur_sems.at[n])
        found = from_rows(cur_recv[n].reshape(DEVICES, 128), line_rank_in, from_line)
        lines_out[n, 0] = found[0:6, 0:128]
        lines_out[n, 1] = found[0:6, 128:256]

    def step(n, carry):
        delayed, worst = carry
        hist = hacc[n] + ht[1] * delayed
        phase = [jnp.sum(mmap[k] * hist, axis=0, keepdims=True) for k in range(6)]
        pieces = jnp.concatenate(
            [p[:, t * 128:(t + 1) * 128] for t in range(2) for p in phase], axis=0
        )
        turned = pltpu.roll(pieces, 64, 1)
        inj[z, n, 0:12] = pieces
        tiles = []
        for t in range(2):
            for h in range(2):
                even, odd = (turned, pieces) if h else (pieces, turned)
                rows = [
                    jnp.where(lane < 64, even[t * 6 + 2 * u:t * 6 + 2 * u + 1], odd[t * 6 + 2 * u + 1:t * 6 + 2 * u + 2])
                    for u in range(3)
                ]
                high, low = split(jnp.concatenate(rows, axis=1))
                both = dot_nt(jnp.concatenate([high, low], axis=0), solve[2 * t + h])
                both = both[0:1] + both[1:2]
                tiles += [
                    both[:, u * 128:(u + 1) * 128] + both[:, 384 + u * 128:512 + u * 128]
                    + v0[u, 2 * t + h, pl.ds(n, 1), :]
                    for u in range(3)
                ]
        volts = jnp.concatenate(tiles, axis=0)
        swung = pltpu.roll(volts, 64, 1)
        modal = jnp.zeros((8, ENDS), F32)
        for k in range(6):
            left, right = (swung, volts) if k % 2 else (volts, swung)
            row = jnp.concatenate(
                [
                    jnp.where(
                        lane < 64, left[6 * t + k // 2:6 * t + k // 2 + 1], right[6 * t + 3 + k // 2:6 * t + 4 + k // 2]
                    )
                    for t in range(2)
                ], axis=1
            )
            modal = modal + mmap[k] * row
        charac = cacc[n] + g[0] * modal
        wave = 2.0 * charac - hist

        @pl.when(n < STEPS - 1)
        def _waves():
            wave_send[n] = (to_rows(wave, peer_rank, to_peer) + flag_lane)[:, None, :]
            send_all(lambda d: wave_send.at[n, d], wave_recv.at[n, me], wave_sems.at[0, n], wave_sems.at[1, n])
            wave_recv[n, me] = wave_send[n, me]

        cur_send[n] = to_rows(charac - hist, line_rank, to_line)[:, None, :]
        send_all(lambda d: cur_send.at[n, d], cur_recv.at[n, me], cur_sems.at[STEPS + n], cur_sems.at[n])
        cur_recv[n, me] = cur_send[n, me]

        @pl.when(lax.rem(n, 4) == 3)
        def _injections():
            part = inj.at[z, pl.ds(n - 3, 4)]
            for k in range(1, 8):
                nz = lax.rem(z + k, 8)
                pltpu.make_async_remote_copy(
                    src_ref=part, dst_ref=part, send_sem=inj_sems.at[0], recv_sem=inj_sems.at[1],
                    device_id=(i, nz), device_id_type=MESH,
                ).start()

        for k in range(2, STEPS):
            hacc[n + k - 1] = hacc[n + k - 1] + ht[k] * delayed
        for k in range(1, STEPS):
            cacc[n + k] = cacc[n + k] + g[k] * modal

        @pl.when(n > 0)
        def _lines():
            take_currents(n - 1)

        last = jnp.minimum(n, STEPS - 2)

        @pl.when(n < STEPS - 1)
        def _arrive():
            drain(wave_recv.at[n, pl.ds(0, DEVICES - 1)], wave_sems.at[1, n])

        rows = wave_recv[last].reshape(DEVICES, 128)
        worst = jnp.maximum(worst, jnp.max(rows[:, 127:128], axis=0, keepdims=True))
        return from_rows(rows, peer_rank_in, from_peer), worst

    delayed, worst = lax.fori_loop(0, STEPS, step, (jnp.zeros((8, ENDS), F32), jnp.zeros((1, 1), F32)))
    flag_out[...] = worst

    drain(inj.at[pl.ds(0, 7)], inj_sems.at[1])

    def finish(a, carry):
        for t in range(2):
            tiles = [inj[a, :, t * 6 + k, :] for k in range(6)]
            for h in range(2):
                s = a * 4 + t * 2 + h
                left = []
                for u in range(3):
                    even, odd = tiles[2 * u], tiles[2 * u + 1]
                    if h == 0:
                        left.append(jnp.where(lane < 64, even, pltpu.roll(odd, 64, 1)))
                    else:
                        left.append(jnp.where(lane < 64, pltpu.roll(even, 64, 1), odd))
                high, low = split(jnp.concatenate(left, axis=1))
                both = dot_nt(jnp.concatenate([high, low], axis=0), fixed[s])
                both = both[:STEPS] + both[STEPS:]
                total = still[s] + both[:, :128] + both[:, 128:]
                live = lane + z * 128 < counts[s]
                volts_out[:, pl.ds(s, 1), :] = jnp.where(live, total, 0.0)[:, None, :]
        return carry

    lax.fori_loop(0, 8, finish, 0)
    take_currents(STEPS - 1)

    drain(code_send.at[pl.ds(0, DEVICES - 1)], code_sems.at[0])
    drain(table_send.at[pl.ds(0, DEVICES - 8)], table_sems.at[0])
    drain(port_send.at[pl.ds(0, 7)], port_sems.at[0])
    drain(inj.at[pl.ds(0, 7)], inj_sems.at[0])

    def sent(n, carry):
        drain(cur_send.at[n, pl.ds(0, DEVICES - 1)], cur_sems.at[STEPS + n])

        @pl.when(n < STEPS - 1)
        def _wave():
            drain(wave_send.at[n, pl.ds(0, DEVICES - 1)], wave_sems.at[0, n])
        return carry

    lax.fori_loop(0, STEPS, sent, 0)

    @pl.when(z >= 4)
    def _relayed():
        drain(relay, relay_sems.at[2])

    @pl.when(z < 3)
    def _sent():
        drain(still.at[pl.ds(0, 28)], v0_sems.at[3])
        drain(inverses.at[pl.ds(0, 28), :, pl.ds(0, 384)], block_sems.at[3])


def run_steps(*operands):
    vm = pl.BlockSpec(memory_space=pltpu.VMEM)
    dma = pltpu.SemaphoreType.DMA
    rows = (STEPS, DEVICES, 1, 128)
    return pl.pallas_call(
        steps_kernel,
        out_shape=(
            jax.ShapeDtypeStruct((STEPS, 32, 128), F32),
            jax.ShapeDtypeStruct((STEPS, 2, 6, 128), F32),
            jax.ShapeDtypeStruct((1, 1), F32),
        ),
        in_specs=[pl.BlockSpec(memory_space=pl.ANY), pl.BlockSpec(memory_space=pltpu.SMEM)] + [vm] * (len(operands) - 2),
        out_specs=(vm, vm, vm),
        scratch_shapes=[
            pltpu.VMEM((2, 6, 30, 128), F32),
            pltpu.VMEM((2, 6, 30, 128), F32),
            pltpu.VMEM((6, 30, 128), F32),
            pltpu.VMEM((6, 30, 128), F32),
            pltpu.VMEM((STEPS, 6, 128), F32),
            pltpu.VMEM((64, 8, ENDS), F32),
            pltpu.VMEM((DEVICES, 1, 128), F32),
            pltpu.VMEM((DEVICES, 1, 128), F32),
            pltpu.VMEM((DEVICES, 8, 512), F32),
            pltpu.VMEM((DEVICES, 8, 512), F32),
            pltpu.VMEM((8, PACK, 512), F32),
            pltpu.VMEM((8, PACK, 512), F32),
            pltpu.VMEM((2, 4, 128, 1024), F32),
            pltpu.VMEM((32, 256, 384), BF16),
            pltpu.VMEM((32, STEPS, 128), F32),
            pltpu.VMEM((3, 4, STEPS, 128), F32),
            pltpu.VMEM((3, 4, 128, 384), F32),
            pltpu.VMEM((4, 128, 384), F32),
            pltpu.VMEM((4, 768, 384), BF16),
            pltpu.VMEM((6, 8, ENDS), F32),
            pltpu.VMEM((32, 8, ENDS), F32),
            pltpu.VMEM((32, 8, ENDS), F32),
            pltpu.VMEM((STEPS, 8, ENDS), F32),
            pltpu.VMEM((STEPS, 8, ENDS), F32),
            pltpu.VMEM((DEVICES, ENDS), BF16),
            pltpu.VMEM((ENDS, DEVICES), BF16),
            pltpu.VMEM((DEVICES, ENDS), BF16),
            pltpu.VMEM((ENDS, DEVICES), BF16),
            pltpu.VMEM(rows, F32),
            pltpu.VMEM(rows, F32),
            pltpu.VMEM(rows, F32),
            pltpu.VMEM(rows, F32),
            pltpu.VMEM((8, STEPS, 16, 128), F32),
            dma((2,)), dma((2,)), dma((2,)), dma((2,)), dma((4,)), dma((4,)), dma((3,)), dma((1,)), dma((2, STEPS)),
            dma((2 * STEPS,)), dma((2,)),
        ],
        compiler_params=pltpu.CompilerParams(collective_id=0, has_side_effects=True, vmem_limit_bytes=VMEM_CAP),
        name="transient_steps",
    )(*operands)


def body(
    inverses, node_counts, sources, port_slot, end_slot, modal_map, delay_steps, wave_buffer, yc_decay, yc_residue,
    yc_direct, yc_state, prop_decay, prop_residue, prop_state,
):
    volts, lines, flag = run_steps(
        inverses, node_counts, sources, port_slot.reshape(1, -1), end_slot.reshape(1, -1), modal_map, delay_steps,
        wave_buffer, yc_decay, yc_residue, yc_direct, yc_state.transpose(1, 2, 0, 3), prop_decay, prop_residue,
        prop_state.transpose(1, 2, 0, 3),
    )

    def quick(_):
        return volts, lines

    def general(_):
        return general_body(
            inverses, node_counts, sources, port_slot, end_slot, modal_map, delay_steps, wave_buffer, yc_decay,
            yc_residue, yc_direct, yc_state, prop_decay, prop_residue, prop_state,
        )

    return lax.cond(flag[0, 0] > 0.0, general, quick, 0)


def read_delayed(extended, delay_steps, step_index, buffer_len):
    read_at = buffer_len + step_index - delay_steps
    depth = jnp.arange(extended.shape[2], dtype=jnp.int32)
    picker = (depth[None, :, None] == read_at[:, None, :]).astype(extended.dtype)
    return jnp.sum(extended * picker[None], axis=2)


def move_back(outgoing):
    returned = lax.all_to_all(outgoing, ("net", "line"), split_axis=1, concat_axis=1, tiled=True)
    return returned


def move_forward(sending):
    arrived = lax.all_to_all(sending, ("net", "line"), split_axis=1, concat_axis=1, tiled=True)
    return arrived


def general_body(
    inverses,
    node_counts,
    sources,
    port_slot,
    end_slot,
    modal_map,
    delay_steps,
    wave_buffer,
    yc_decay,
    yc_residue,
    yc_direct,
    yc_state,
    prop_decay,
    prop_residue,
    prop_state,
):
    net_size = lax.axis_size("net")
    line_size = lax.axis_size("line")
    device_count = net_size * line_size
    sub_count, row_count, node_total = inverses.shape
    step_count = sources.shape[0]
    port_cols = port_slot.shape[1]
    mode_count = modal_map.shape[0]
    line_count = end_slot.shape[1]
    buffer_len = wave_buffer.shape[2]
    port_total = port_cols * line_size
    slot_cap = max(2, 4 * sub_count * port_cols // device_count)
    slot_width = device_count * slot_cap
    line_pos = lax.axis_index("line")
    row_ids = line_pos * row_count + jnp.arange(row_count, dtype=jnp.int32)
    live_mask = row_ids[None, :] < node_counts[:, None]
    port_flat = port_slot.reshape(-1)
    end_flat = end_slot.reshape(-1)
    used_nodes = port_total * mode_count
    first_port = line_pos * port_cols
    extended = jnp.concatenate(
        [wave_buffer, jnp.zeros((2, mode_count, step_count, line_count), jnp.float32)], axis=2
    )
    volts_init = jnp.zeros((step_count, sub_count, row_count), jnp.float32)
    currents_init = jnp.zeros((step_count, 2, mode_count, line_count), jnp.float32)

    def advance(step_index, carried):
        yc_now, prop_now, extended, volts_acc, currents_acc = carried
        delayed = read_delayed(extended, delay_steps, step_index, buffer_len)
        prop_now = prop_decay[None] * prop_now + prop_residue[None] * delayed[::-1][:, :, None, :]
        history = jnp.sum(prop_now, axis=2)
        history_phase = jnp.sum(modal_map[None] * history[:, None], axis=2)
        outgoing = (
            jnp.zeros((mode_count, slot_width), jnp.float32)
            .at[:, end_flat]
            .set(history_phase.transpose(1, 0, 2).reshape(mode_count, 2 * line_count))
        )
        returned = move_back(outgoing)
        own_ports = (
            returned[:, port_flat]
            .reshape(mode_count, sub_count, port_cols)
            .transpose(1, 2, 0)
            .reshape(sub_count, port_cols * mode_count)
        )
        port_currents = lax.all_gather(own_ports, "line", axis=1, tiled=True)
        port_currents = (
            port_currents.reshape(sub_count, port_total, mode_count)
            .transpose(0, 2, 1)
            .reshape(sub_count, used_nodes)
        )
        source_now = lax.dynamic_index_in_dim(sources, step_index, 0, keepdims=False)
        injection = source_now + jnp.pad(port_currents, ((0, 0), (0, node_total - used_nodes)))
        solved = jnp.einsum("src,sc->sr", inverses, injection, precision=lax.Precision.HIGHEST)
        solved = jnp.where(live_mask, solved, 0.0)
        gathered = lax.all_gather(solved, "line", axis=1, tiled=True)
        by_mode = gathered[:, :used_nodes].reshape(sub_count, mode_count, port_total)
        own_volts = lax.dynamic_slice_in_dim(by_mode, first_port, port_cols, 2)
        own_volts = own_volts.transpose(1, 0, 2).reshape(mode_count, sub_count * port_cols)
        sending = jnp.zeros((mode_count, slot_width), jnp.float32).at[:, port_flat].set(own_volts)
        arrived = move_forward(sending)
        end_volts = arrived[:, end_flat].reshape(mode_count, 2, line_count)
        modal_volts = jnp.sum(modal_map[:, :, None, :] * end_volts[:, None], axis=0).transpose(
            1, 0, 2
        )
        yc_now = yc_decay[None] * yc_now + yc_residue[None] * modal_volts[:, :, None, :]
        charac = yc_direct[None] * modal_volts + jnp.sum(yc_now, axis=2)
        current = charac - history
        wave_out = 2.0 * charac - history
        extended = lax.dynamic_update_slice_in_dim(
            extended, wave_out[:, :, None, :], buffer_len + step_index, 2
        )
        volts_acc = lax.dynamic_update_slice_in_dim(volts_acc, solved[None], step_index, 0)
        currents_acc = lax.dynamic_update_slice_in_dim(currents_acc, current[None], step_index, 0)
        return (yc_now, prop_now, extended, volts_acc, currents_acc)

    final = lax.fori_loop(
        0, step_count, advance, (yc_state, prop_state, extended, volts_init, currents_init)
    )
    return (final[3], final[4])


def solution(mesh):
    placed = (
        P("net", "line", None),
        P("net"),
        P(None, "net", None),
        P("net", "line"),
        P(None, ("net", "line")),
        P(None, None, ("net", "line")),
        P(None, ("net", "line")),
        P(None, None, None, ("net", "line")),
        P(None, None, ("net", "line")),
        P(None, None, ("net", "line")),
        P(None, ("net", "line")),
        P(None, None, None, ("net", "line")),
        P(None, None, ("net", "line")),
        P(None, None, ("net", "line")),
        P(None, None, None, ("net", "line")),
    )
    return jax.shard_map(
        body,
        mesh=mesh,
        in_specs=placed,
        out_specs=(P(None, "net", "line"), P(None, None, None, ("net", "line"))),
        check_vma=False,
    )
```
